32 devices in a mesh: bx: 4 (over y, x), by: 8 (over z, core).
Axes of the slice: x: 2, y: 2, z: 4, core: 2. Of those that a mesh axis runs over, the one named last changes fastest.
Arguments:
- populations: float32 [27, 64, 128, 128], P(None, 'bx', 'by'), as said below
- block_level: int32 [256], replicated, may hold values 0 or 1
- new_slot: int32 [256], P(('bx', 'by')), may hold values from 0 to 255, as said below
Outputs:
- density: float32 [256, 4096], P(('bx', 'by'))
- velocity: float32 [3, 256, 4096], P(None, ('bx', 'by'))
The draws below stay inside these ranges and needn't reach their ends.
Inputs may be any that keep to these rules, and one draw needn't show every extreme that they name: `populations`: every population is positive. new_slot is a permutation; slot s belongs to device s // 8 in the curve order, which is the order of bx+by. Every block stays at its slot or moves to the next or the previous device in that order; at most one block of a device goes to each of those two devices, and it takes the slot of the block that crosses the same cut the other way. Some cut is crossed in every draw.
All inputs are finite; a program needn't handle non-finite values.
Results may differ from the reference program's by a relative error of at most 0.0003.
Values sent between devices are 32-bit elements; how exact they have to be, the bound alone decides.
A program may use at most 192 MiB of HBM per device.

```python
import math
import jax
import jax.numpy as jnp
import numpy as np
from jax import lax

BLK_EDGE = 16
BLK_DEV = 8
STEPS = 1
NX = 64
NY = 128
NZ = 128
NBLK = 256
CELLS = 4096
N_BX = 4
N_BY = 8


def draw_populations(key, part):
    key = jax.random.fold_in(key, 5)
    key_rho, key_vel, key_noise = jax.random.split(key, 3)
    shape = (NX, NY, NZ)
    density = jax.random.uniform(key_rho, shape, jnp.float32, 0.8, 1.2)
    velocity = 0.04 * jnp.clip(jax.random.normal(key_vel, (3,) + shape, jnp.float32), -3.0, 3.0)
    table = np.array([[first, second, third] for first in (-1, 0, 1) for second in (-1, 0, 1) for third in (-1, 0, 1)], dtype=np.float32)
    squares = np.sum(table * table, axis=1)
    weights = np.where(squares == 0, 8.0 / 27, np.where(squares == 1, 2.0 / 27, np.where(squares == 2, 1.0 / 54, 1.0 / 216))).astype(np.float32)
    comp_x = jnp.asarray(table[:, 0]).reshape(27, 1, 1, 1)
    comp_y = jnp.asarray(table[:, 1]).reshape(27, 1, 1, 1)
    comp_z = jnp.asarray(table[:, 2]).reshape(27, 1, 1, 1)
    projected = comp_x * velocity[0] + comp_y * velocity[1] + comp_z * velocity[2]
    speed_sq = velocity[0] * velocity[0] + velocity[1] * velocity[1] + velocity[2] * velocity[2]
    balance = jnp.asarray(weights).reshape(27, 1, 1, 1) * density * (1.0 + 3.0 * projected + 4.5 * projected * projected - 1.5 * speed_sq)
    noise = jax.random.uniform(key_noise, (27,) + shape, jnp.float32, -0.15, 0.15)
    return (balance * (1.0 + noise)).astype(jnp.float32)


def draw_new_slot(key, part):
    key = jax.random.fold_in(key, 11)
    key_cut, key_slots, key_force = jax.random.split(key, 3)
    devices = NBLK // BLK_DEV
    cut_on = jax.random.randint(key_cut, (devices - 1,), 0, 2)
    forced = jax.random.randint(key_force, (), 0, devices - 1)
    cut_on = jnp.where(jnp.arange(devices - 1) == forced, 1, cut_on)
    orders = jax.vmap(lambda single: jax.random.permutation(single, BLK_DEV))(jax.random.split(key_slots, devices))
    left_slot = orders[:, 0]
    right_slot = orders[:, 1]
    cuts = jnp.arange(devices - 1, dtype=jnp.int32)
    lower = cuts * BLK_DEV + right_slot[:-1]
    upper = (cuts + 1) * BLK_DEV + left_slot[1:]
    base = jnp.arange(NBLK, dtype=jnp.int32)
    moved = base.at[lower].set(jnp.where(cut_on == 1, upper, lower))
    moved = moved.at[upper].set(jnp.where(cut_on == 1, lower, upper))
    return moved.astype(jnp.int32)


def touch_ends(result, stream_key, low, top_value):
    longest = result.shape.index(max(result.shape))
    spots = []
    for shift in (0, 1):
        where = [jax.random.randint(jax.random.fold_in(stream_key, axis), (), 0, length) for axis, length in enumerate(result.shape)]
        where[longest] = (where[longest] + shift) % result.shape[longest]
        spots.append(tuple(where))
    return result.at[spots[0]].set(low).at[spots[1]].set(top_value)


def setup_inputs(seed: int = 0) -> dict:
    seeds = jax.random.split(jax.random.key(seed), 4)
    return {
        "populations": draw_populations(jax.random.fold_in(seeds[3], 71), 0),
        "block_level": touch_ends((jax.random.randint(seeds[1], (NBLK,), 0, 5) < 1).astype(jnp.int32), jax.random.fold_in(seeds[1], 1), 0, 1),
        "new_slot": draw_new_slot(jax.random.fold_in(seeds[3], 71), 0),
    }


lattice_vel = np.array([[first, second, third] for first in (-1, 0, 1) for second in (-1, 0, 1) for third in (-1, 0, 1)], dtype=np.float32)
lattice_sq = np.sum(lattice_vel * lattice_vel, axis=1)
lattice_wts = np.where(lattice_sq == 0, 8.0 / 27, np.where(lattice_sq == 1, 2.0 / 27, np.where(lattice_sq == 2, 1.0 / 54, 1.0 / 216))).astype(np.float32)
stress_table = np.stack([lattice_vel[:, first] * lattice_vel[:, second] for first in range(3) for second in range(3)]).astype(np.float32)
tau_coarse = 0.56
tau_fine = 0.62
scale_to_fine = tau_fine / (2.0 * tau_coarse)
scale_to_coarse = 2.0 * tau_coarse / tau_fine
smagorinsky = 18.0 * math.sqrt(2.0) * 0.17 * 0.17

def cell_moments(states):
    density = lax.optimization_barrier(jnp.sum(states, axis=0))
    momentum = jnp.einsum('ia,i...->a...', jnp.asarray(lattice_vel), states, precision=lax.Precision.HIGHEST)
    return (density, momentum / density)

def equilibrium(density, velocity):
    projected = jnp.einsum('ia,a...->i...', jnp.asarray(lattice_vel), velocity, precision=lax.Precision.HIGHEST)
    speed_sq = lax.optimization_barrier(jnp.sum(velocity * velocity, axis=0))
    weights = jnp.asarray(lattice_wts).reshape((27,) + (1,) * density.ndim)
    return weights * density * (1.0 + 3.0 * projected + 4.5 * projected * projected - 1.5 * speed_sq)

def relax_cells(states, fine_cells, active_cells):
    density, velocity = cell_moments(states)
    balance = equilibrium(density, velocity)
    departure = states - balance
    stress = jnp.einsum('ki,i...->k...', jnp.asarray(stress_table), departure, precision=lax.Precision.HIGHEST)
    stress_norm = jnp.sqrt(lax.optimization_barrier(jnp.sum(stress * stress, axis=0)))
    base_time = jnp.where(fine_cells, tau_fine, tau_coarse)
    relax_time = 0.5 * (base_time + jnp.sqrt(base_time * base_time + smagorinsky * stress_norm / density))
    relaxed = jnp.where(active_cells, states - departure / relax_time, states)
    factor = jnp.where(fine_cells, scale_to_coarse, scale_to_fine)
    rescaled = balance + factor * (relaxed - balance)
    return (relaxed, rescaled)

def reference(populations, block_level, new_slot):
    levels = block_level.reshape(N_BX, N_BY, BLK_DEV)
    cell_level = jnp.repeat(jnp.repeat(jnp.repeat(levels, BLK_EDGE, 0), BLK_EDGE, 1), BLK_EDGE, 2)
    fine_cells = cell_level == 1
    crossing = jnp.stack([jnp.roll(cell_level, (-int(offset[0]), -int(offset[1]), -int(offset[2])), axis=(0, 1, 2)) != cell_level for offset in lattice_vel])
    every = jnp.ones_like(fine_cells)
    state = populations
    for step in range(STEPS):
        for substep in range(2):
            active_cells = fine_cells if substep == 0 else every
            relaxed, rescaled = relax_cells(state, fine_cells, active_cells)
            outgoing = jnp.where(crossing, rescaled, relaxed)
            read = jnp.stack([jnp.roll(outgoing[direction], (int(lattice_vel[direction][0]), int(lattice_vel[direction][1]), int(lattice_vel[direction][2])), axis=(0, 1, 2)) for direction in range(27)])
            state = jnp.where(active_cells, read, state)
    density, velocity = cell_moments(state)
    fields = jnp.concatenate([density[None], velocity], axis=0)
    fields = fields.reshape(4, N_BX, BLK_EDGE, N_BY, BLK_EDGE, BLK_DEV, BLK_EDGE)
    fields = fields.transpose(0, 1, 3, 5, 2, 4, 6).reshape(4, NBLK, CELLS)
    placed = jnp.zeros_like(fields).at[:, new_slot].set(fields)
    return (placed[0], placed[1:4])
```

```python
import functools
import math

import jax
import jax.numpy as jnp
from jax import lax
from jax.experimental import pallas as pl
from jax.experimental.pallas import tpu as pltpu
from jax.sharding import PartitionSpec as P

MESH = pl.DeviceIdType.MESH
TAU_COARSE = 0.56
TAU_FINE = 0.62
TO_FINE = TAU_FINE / (2.0 * TAU_COARSE)
TO_COARSE = 2.0 * TAU_COARSE / TAU_FINE
SMAGORINSKY = 18.0 * math.sqrt(2.0) * 0.17 * 0.17
WEIGHTS = (8.0 / 27, 2.0 / 27, 1.0 / 54, 1.0 / 216)
DIRECTIONS = [(a, b, e) for a in range(3) for b in range(3) for e in range(3)]
SIDES = [(a, b) for a in (0, 2, 1) for b in (1, 0, 2) if (a, b) != (1, 1)]
HALF = [d for d in DIRECTIONS if d > (1, 1, 1)]
PAD = 8


def opposite(direction):
    return tuple(2 - part for part in direction)


def partial_sums(f):
    ends = {(a, b): f[a, b, 0] + f[a, b, 2] for a in range(3) for b in range(3)}
    whole = {key: ends[key] + f[key + (1,)] for key in ends}
    diff = {(a, b): f[a, b, 2] - f[a, b, 0] for a in range(3) for b in range(3)}
    return ends, whole, diff


def first_moments(f):
    ends, whole, diff = partial_sums(f)
    along_x = [whole[a, 0] + whole[a, 1] + whole[a, 2] for a in range(3)]
    y_low = whole[0, 0] + whole[1, 0] + whole[2, 0]
    y_high = whole[0, 2] + whole[1, 2] + whole[2, 2]
    diff_x = [diff[a, 0] + diff[a, 1] + diff[a, 2] for a in range(3)]
    rho = along_x[0] + along_x[1] + along_x[2]
    momentum = (along_x[2] - along_x[0], y_high - y_low, diff_x[0] + diff_x[1] + diff_x[2])
    stress = (ends, whole, diff, along_x, y_low, y_high, diff_x)
    return rho, momentum, stress


def relax(f, base_time, inactive, factor_of):
    rho, (jx, jy, jz), (ends, whole, diff, along_x, y_low, y_high, diff_x) = first_moments(f)
    pxx = along_x[0] + along_x[2]
    pyy = y_low + y_high
    pzz = ends[0, 0]
    for key in list(ends)[1:]:
        pzz = pzz + ends[key]
    pxy = (whole[2, 2] - whole[2, 0]) - (whole[0, 2] - whole[0, 0])
    pxz = diff_x[2] - diff_x[0]
    pyz = (diff[0, 2] + diff[1, 2] + diff[2, 2]) - (diff[0, 0] + diff[1, 0] + diff[2, 0])
    inv = 1.0 / rho
    ux, uy, uz = jx * inv, jy * inv, jz * inv
    third = rho * (1.0 / 3.0)
    pxx = pxx - third - jx * ux
    pyy = pyy - third - jy * uy
    pzz = pzz - third - jz * uz
    pxy = pxy - jx * uy
    pxz = pxz - jx * uz
    pyz = pyz - jy * uz
    off = pxy * pxy + pxz * pxz + pyz * pyz
    norm = jnp.sqrt(pxx * pxx + pyy * pyy + pzz * pzz + (off + off))
    tau = 0.5 * (base_time + jnp.sqrt(base_time * base_time + SMAGORINSKY * norm * inv))
    keep = 1.0 - 1.0 / tau
    if inactive is not None:
        keep = jnp.where(inactive, 1.0, keep)
    rest = 1.0 - 1.5 * (ux * ux + uy * uy + uz * uz)
    scaled = [rho * w for w in WEIGHTS]
    rests = [s * rest for s in scaled]
    squares = [s * 4.5 for s in scaled]
    linear = [s * 3.0 for s in scaled]
    out = {}

    def emit(d, balance):
        out[d] = balance + (f[d] - balance) * (keep * factor_of(d))

    emit((1, 1, 1), rests[0])
    plane = {}
    for a in (1, 2):
        for b in range(3):
            if a == 1 and b == 1:
                plane[a, b] = None
            elif a == 1:
                plane[a, b] = uy if b == 2 else -uy
            else:
                plane[a, b] = ux if b == 1 else (ux + uy if b == 2 else ux - uy)
    for d in HALF:
        a, b, e = d
        level = sum(part != 1 for part in d)
        flat = plane[a, b]
        if flat is None:
            proj = uz
        elif e == 1:
            proj = flat
        else:
            proj = flat + uz if e == 2 else flat - uz
        even = rests[level] + squares[level] * (proj * proj)
        odd = linear[level] * proj
        emit(d, even + odd)
        emit(opposite(d), even - odd)
    return out


def swap_chunks(value, sub, chunk):
    lanes = value.shape[1]
    width = lanes // 8
    for k in (4, 2, 1):
        sub_bit = (sub & k) != 0
        chunk_bit = (chunk & k) != 0
        down = pltpu.roll(pltpu.roll(value, k, 0), lanes - width * k, 1)
        if k == 4:
            value = jnp.where(sub_bit != chunk_bit, down, value)
        else:
            up = pltpu.roll(pltpu.roll(value, 8 - k, 0), width * k, 1)
            value = jnp.where(
                sub_bit & ~chunk_bit, down, jnp.where(~sub_bit & chunk_bit, up, value)
            )
    return value


def kernel(
    sizes,
    level_ref,
    slot_ref,
    pop_ref,
    density_ref,
    velocity_ref,
    held,
    first,
    second,
    factors,
    leave_next,
    leave_prev,
    come_next,
    come_prev,
    load_sem,
    send_sem,
    recv_sem,
    move_send,
    move_recv,
):
    count_x, count_y, size_x, size_y, size_z, blocks = sizes
    halves = size_y // 8
    index_x = lax.axis_index("bx")
    index_y = lax.axis_index("by")
    near_x = [lax.rem(index_x + count_x + a - 1, count_x) for a in range(3)]
    near_y = [lax.rem(index_y + count_y + b - 1, count_y) for b in range(3)]

    loads = []
    parts = load_sem.shape[0]
    step = size_x // parts
    for part in range(parts):
        piece = pl.ds(part * step, step)
        load = pltpu.make_async_copy(pop_ref.at[:, piece], held.at[:, piece], load_sem.at[part])
        load.start()
        loads.append(load)

    barrier = pltpu.get_barrier_semaphore()
    for a, b in SIDES:
        pl.semaphore_signal(
            barrier, inc=1, device_id=(near_x[a], near_y[b]), device_id_type=MESH
        )

    tile = (8, size_z)
    sub = lax.broadcasted_iota(jnp.int32, tile, 0)
    lane = lax.broadcasted_iota(jnp.int32, tile, 1)
    chunk = lane // (size_z // blocks)

    def spread(values, index):
        result = jnp.full(tile, values[0], jnp.int32)
        for n in range(1, len(values)):
            result = jnp.where(index == n, values[n], result)
        return result

    levels = {}
    for a in range(3):
        for b in range(3):
            begin = (near_x[a] * count_y + near_y[b]) * blocks
            flat = spread([level_ref[begin + n] for n in range(blocks)], chunk)
            for e in range(3):
                levels[a, b, e] = pltpu.roll(flat, (1 - e) % size_z, 1) if e != 1 else flat
    own = levels[1, 1, 1]
    fine = own == 1
    coarse = own != 1
    scale = jnp.where(fine, TO_COARSE, TO_FINE)
    base_time = jnp.where(fine, TAU_FINE, TAU_COARSE)
    for edge in range(3):
        for half in range(halves):
            for a, b, e in DIRECTIONS:
                over = a if a == edge and a != 1 else 1
                other = levels[over, 1, e]
                if b == 0 and half == 0:
                    other = jnp.where(sub == 0, levels[over, 0, e], other)
                if b == 2 and half == halves - 1:
                    other = jnp.where(sub == 7, levels[over, 2, e], other)
                factors[edge, half, 9 * a + 3 * b + e] = jnp.where(other != own, scale, 1.0)

    def factor_at(x, half):
        edge = (x + size_x - 1) // size_x + (x + 1) // size_x

        def factor_of(d):
            return factors[edge, half, 9 * d[0] + 3 * d[1] + d[2]]

        return factor_of

    def put(target, x, half, out):
        for d in DIRECTIONS:
            target[d[0], d[1], d[2], x + 1, pl.ds(PAD + 8 * half, 8), :] = out[d]

    def pulled(source, x, half):
        f = {}
        for a, b, e in DIRECTIONS:
            value = source[a, b, e, x + 2 - a, pl.ds(PAD + 8 * half + 1 - b, 8), :]
            f[a, b, e] = pltpu.roll(value, (e - 1) % size_z, 1) if e != 1 else value
        return f

    def held_at(x, half):
        return {
            (a, b, e): held[9 * a + 3 * b + e, x, pl.ds(8 * half, 8), :] for a, b, e in DIRECTIONS
        }

    def exchange(buffer, turn):
        copies = []
        for n, (a, b) in enumerate(SIDES):
            here_x = {0: 1, 2: size_x}
            there_x = {0: size_x + 1, 2: 0}
            here_y = {0: PAD, 2: PAD + size_y - 1}
            there_y = {0: PAD + size_y, 2: PAD - 1}
            dirs_a = pl.ds(a, 1) if a != 1 else pl.ds(0, 3)
            dirs_b = pl.ds(b, 1) if b != 1 else pl.ds(0, 3)
            from_x = pl.ds(here_x[a], 1) if a != 1 else pl.ds(1, size_x)
            into_x = pl.ds(there_x[a], 1) if a != 1 else pl.ds(1, size_x)
            from_y = pl.ds(here_y[b], 1) if b != 1 else pl.ds(PAD, size_y)
            into_y = pl.ds(there_y[b], 1) if b != 1 else pl.ds(PAD, size_y)
            copy = pltpu.make_async_remote_copy(
                src_ref=buffer.at[dirs_a, dirs_b, :, from_x, from_y, :],
                dst_ref=buffer.at[dirs_a, dirs_b, :, into_x, into_y, :],
                send_sem=send_sem.at[turn, n],
                recv_sem=recv_sem.at[turn, n],
                device_id=(near_x[a], near_y[b]),
                device_id_type=MESH,
            )
            copy.start()
            copies.append(copy)
        return copies

    def first_body(x, carry):
        for half in range(halves):
            put(first, x, half, relax(held_at(x, half), base_time, coarse, factor_at(x, half)))
        return carry

    def second_body(x, carry):
        for half in range(halves):
            kept, moved = held_at(x, half), pulled(first, x, half)
            f = {d: jnp.where(fine, moved[d], kept[d]) for d in DIRECTIONS}
            put(second, x, half, relax(f, base_time, None, factor_at(x, half)))
        return carry

    for part in range(parts):
        loads[part].wait()
        lax.fori_loop(part * step, (part + 1) * step, first_body, 0)

    pl.semaphore_wait(barrier, len(SIDES))
    copies = exchange(first, 0)
    for copy in copies:
        copy.wait()
    lax.fori_loop(0, size_x, second_body, 0)
    copies = exchange(second, 1)
    for copy in copies:
        copy.wait()

    curve = index_x * count_y + index_y
    home = spread([slot_ref[n] // blocks for n in range(blocks)], sub)
    to_next = home == curve + 1
    to_prev = home == curve - 1

    def last_body(x, carry):
        for half in range(halves):
            rho, momentum, _ = first_moments(pulled(second, x, half))
            inv = 1.0 / rho
            at = x * halves + half
            cells = pl.ds(pl.multiple_of(at * size_z, size_z), size_z)
            fields = [rho] + [part * inv for part in momentum]
            for n, field in enumerate(fields):
                field = swap_chunks(field, sub, chunk)
                if n == 0:
                    density_ref[:, cells] = field
                else:
                    velocity_ref[n - 1, :, cells] = field
                for mask, buffer in ((to_next, leave_next), (to_prev, leave_prev)):
                    buffer[n, pl.ds(at, 1), :] = jnp.sum(
                        jnp.where(mask, field, 0.0), axis=0, keepdims=True
                    )
        return carry

    lax.fori_loop(0, size_x, last_body, 0)

    after_x = lax.rem(index_x + (index_y + 1) // count_y, count_x)
    before_x = lax.rem(index_x + count_x - (count_y - index_y) // count_y, count_x)
    moves = []
    for n, (source, target, device) in enumerate(
        (
            (leave_next, come_prev, (after_x, near_y[2])),
            (leave_prev, come_next, (before_x, near_y[0])),
        )
    ):
        copy = pltpu.make_async_remote_copy(
            src_ref=source,
            dst_ref=target,
            send_sem=move_send.at[n],
            recv_sem=move_recv.at[n],
            device_id=device,
            device_id_type=MESH,
        )
        copy.start()
        moves.append(copy)
    for copy in moves:
        copy.wait()

    def place_body(x, carry):
        for half in range(halves):
            at = x * halves + half
            cells = pl.ds(pl.multiple_of(at * size_z, size_z), size_z)
            for n in range(4):
                old = density_ref[:, cells] if n == 0 else velocity_ref[n - 1, :, cells]
                up = jnp.broadcast_to(come_prev[n, pl.ds(at, 1), :], tile)
                down = jnp.broadcast_to(come_next[n, pl.ds(at, 1), :], tile)
                new = jnp.where(to_prev, up, jnp.where(to_next, down, old))
                if n == 0:
                    density_ref[:, cells] = new
                else:
                    velocity_ref[n - 1, :, cells] = new
        return carry

    lax.fori_loop(0, size_x, place_body, 0)


def on_device(populations, block_level, new_slot):
    _, size_x, size_y, size_z = populations.shape
    blocks = new_slot.shape[0]
    sizes = (lax.axis_size("bx"), lax.axis_size("by"), size_x, size_y, size_z, blocks)
    cells = size_x * size_y * size_z // blocks
    tiles = cells // size_z
    padded = pltpu.VMEM((3, 3, 3, size_x + 2, size_y + 2 * PAD, size_z), jnp.float32)
    moving = pltpu.VMEM((4, tiles, size_z), jnp.float32)
    return pl.pallas_call(
        functools.partial(kernel, sizes),
        out_shape=(
            jax.ShapeDtypeStruct((blocks, cells), jnp.float32),
            jax.ShapeDtypeStruct((3, blocks, cells), jnp.float32),
        ),
        in_specs=[
            pl.BlockSpec(memory_space=pltpu.SMEM),
            pl.BlockSpec(memory_space=pltpu.SMEM),
            pl.BlockSpec(memory_space=pl.ANY),
        ],
        out_specs=[pl.BlockSpec(memory_space=pltpu.VMEM)] * 2,
        scratch_shapes=[
            pltpu.VMEM(populations.shape, jnp.float32),
            padded,
            padded,
            pltpu.VMEM((3, size_y // 8, 27, 8, size_z), jnp.float32),
            moving,
            moving,
            moving,
            moving,
            pltpu.SemaphoreType.DMA((4,)),
            pltpu.SemaphoreType.DMA((2, len(SIDES))),
            pltpu.SemaphoreType.DMA((2, len(SIDES))),
            pltpu.SemaphoreType.DMA((2,)),
            pltpu.SemaphoreType.DMA((2,)),
        ],
        compiler_params=pltpu.CompilerParams(
            collective_id=0, has_side_effects=True, vmem_limit_bytes=40 * 1024 * 1024
        ),
    )(block_level, new_slot, populations)


def solution(mesh):
    in_specs = (P(None, "bx", "by", None), P(), P(("bx", "by")))
    out_specs = (P(("bx", "by"), None), P(None, ("bx", "by"), None))
    return jax.shard_map(
        on_device, mesh=mesh, in_specs=in_specs, out_specs=out_specs, check_vma=False
    )
```

```python
import functools
import math

import jax
import jax.numpy as jnp
from jax import lax
from jax.experimental import pallas as pl
from jax.experimental.pallas import tpu as pltpu
from jax.sharding import PartitionSpec as P

MESH = pl.DeviceIdType.MESH
TAU_COARSE = 0.56
TAU_FINE = 0.62
TO_FINE = TAU_FINE / (2.0 * TAU_COARSE)
TO_COARSE = 2.0 * TAU_COARSE / TAU_FINE
SMAGORINSKY = 18.0 * math.sqrt(2.0) * 0.17 * 0.17
WEIGHTS = (8.0 / 27, 2.0 / 27, 1.0 / 54, 1.0 / 216)
DIRECTIONS = [(a, b, e) for a in range(3) for b in range(3) for e in range(3)]
SIDES = [(a, b) for a in (0, 2, 1) for b in (1, 0, 2) if (a, b) != (1, 1)]
HALF = [d for d in DIRECTIONS if d > (1, 1, 1)]
PAD = 8


def opposite(direction):
    return tuple(2 - part for part in direction)


def partial_sums(f):
    ends = {(a, b): f[a, b, 0] + f[a, b, 2] for a in range(3) for b in range(3)}
    whole = {key: ends[key] + f[key + (1,)] for key in ends}
    diff = {(a, b): f[a, b, 2] - f[a, b, 0] for a in range(3) for b in range(3)}
    return ends, whole, diff


def first_moments(f):
    ends, whole, diff = partial_sums(f)
    along_x = [whole[a, 0] + whole[a, 1] + whole[a, 2] for a in range(3)]
    y_low = whole[0, 0] + whole[1, 0] + whole[2, 0]
    y_high = whole[0, 2] + whole[1, 2] + whole[2, 2]
    diff_x = [diff[a, 0] + diff[a, 1] + diff[a, 2] for a in range(3)]
    rho = along_x[0] + along_x[1] + along_x[2]
    momentum = (along_x[2] - along_x[0], y_high - y_low, diff_x[0] + diff_x[1] + diff_x[2])
    stress = (ends, whole, diff, along_x, y_low, y_high, diff_x)
    return rho, momentum, stress


def relax(f, base_time, inactive, factor_of):
    rho, (jx, jy, jz), (ends, whole, diff, along_x, y_low, y_high, diff_x) = first_moments(f)
    pxx = along_x[0] + along_x[2]
    pyy = y_low + y_high
    pzz = ends[0, 0]
    for key in list(ends)[1:]:
        pzz = pzz + ends[key]
    pxy = (whole[2, 2] - whole[2, 0]) - (whole[0, 2] - whole[0, 0])
    pxz = diff_x[2] - diff_x[0]
    pyz = (diff[0, 2] + diff[1, 2] + diff[2, 2]) - (diff[0, 0] + diff[1, 0] + diff[2, 0])
    inv = 1.0 / rho
    ux, uy, uz = jx * inv, jy * inv, jz * inv
    third = rho * (1.0 / 3.0)
    pxx = pxx - third - jx * ux
    pyy = pyy - third - jy * uy
    pzz = pzz - third - jz * uz
    pxy = pxy - jx * uy
    pxz = pxz - jx * uz
    pyz = pyz - jy * uz
    off = pxy * pxy + pxz * pxz + pyz * pyz
    norm = jnp.sqrt(pxx * pxx + pyy * pyy + pzz * pzz + (off + off))
    tau = 0.5 * (base_time + jnp.sqrt(base_time * base_time + SMAGORINSKY * norm * inv))
    keep = 1.0 - 1.0 / tau
    if inactive is not None:
        keep = jnp.where(inactive, 1.0, keep)
    rest = 1.0 - 1.5 * (ux * ux + uy * uy + uz * uz)
    scaled = [rho * w for w in WEIGHTS]
    rests = [s * rest for s in scaled]
    squares = [s * 4.5 for s in scaled]
    linear = [s * 3.0 for s in scaled]
    out = {}

    def emit(d, balance):
        out[d] = balance + (f[d] - balance) * (keep * factor_of(d))

    emit((1, 1, 1), rests[0])
    plane = {}
    for a in (1, 2):
        for b in range(3):
            if a == 1 and b == 1:
                plane[a, b] = None
            elif a == 1:
                plane[a, b] = uy if b == 2 else -uy
            else:
                plane[a, b] = ux if b == 1 else (ux + uy if b == 2 else ux - uy)
    for d in HALF:
        a, b, e = d
        level = sum(part != 1 for part in d)
        flat = plane[a, b]
        if flat is None:
            proj = uz
        elif e == 1:
            proj = flat
        else:
            proj = flat + uz if e == 2 else flat - uz
        even = rests[level] + squares[level] * (proj * proj)
        odd = linear[level] * proj
        emit(d, even + odd)
        emit(opposite(d), even - odd)
    return out


def swap_chunks(value, sub, chunk):
    lanes = value.shape[1]
    width = lanes // 8
    for k in (4, 2, 1):
        sub_bit = (sub & k) != 0
        chunk_bit = (chunk & k) != 0
        down = pltpu.roll(pltpu.roll(value, k, 0), lanes - width * k, 1)
        if k == 4:
            value = jnp.where(sub_bit != chunk_bit, down, value)
        else:
            up = pltpu.roll(pltpu.roll(value, 8 - k, 0), width * k, 1)
            value = jnp.where(
                sub_bit & ~chunk_bit, down, jnp.where(~sub_bit & chunk_bit, up, value)
            )
    return value


def kernel(
    sizes,
    level_hbm,
    slot_hbm,
    pop_ref,
    density_ref,
    velocity_ref,
    level_ref,
    slot_ref,
    held,
    first,
    second,
    factors,
    leave_next,
    leave_prev,
    come_next,
    come_prev,
    load_sem,
    send_sem,
    recv_sem,
    move_send,
    move_recv,
):
    count_x, count_y, size_x, size_y, size_z, blocks = sizes
    halves = size_y // 8
    index_x = lax.axis_index("bx")
    index_y = lax.axis_index("by")
    near_x = [lax.rem(index_x + count_x + a - 1, count_x) for a in range(3)]
    near_y = [lax.rem(index_y + count_y + b - 1, count_y) for b in range(3)]

    middle = size_x // 2
    pieces = ((0, 1), (size_x - 1, size_x), (1, middle), (middle, size_x - 1))
    loads = []
    for n, (low, high) in enumerate(pieces):
        piece = pl.ds(low, high - low)
        load = pltpu.make_async_copy(pop_ref.at[:, piece], held.at[:, piece], load_sem.at[n])
        load.start()
        loads.append(load)
    tables = [
        pltpu.make_async_copy(level_hbm, level_ref, load_sem.at[len(pieces)]),
        pltpu.make_async_copy(slot_hbm, slot_ref, load_sem.at[len(pieces) + 1]),
    ]
    for table in tables:
        table.start()

    barrier = pltpu.get_barrier_semaphore()
    for a, b in SIDES:
        pl.semaphore_signal(
            barrier, inc=1, device_id=(near_x[a], near_y[b]), device_id_type=MESH
        )

    tile = (8, size_z)
    sub = lax.broadcasted_iota(jnp.int32, tile, 0)
    lane = lax.broadcasted_iota(jnp.int32, tile, 1)
    chunk = lane // (size_z // blocks)

    def spread(values, index):
        result = jnp.full(tile, values[0], jnp.int32)
        for n in range(1, len(values)):
            result = jnp.where(index == n, values[n], result)
        return result

    for table in tables:
        table.wait()
    levels = {}
    for a in range(3):
        for b in range(3):
            begin = (near_x[a] * count_y + near_y[b]) * blocks
            flat = spread([level_ref[begin + n] for n in range(blocks)], chunk)
            for e in range(3):
                levels[a, b, e] = pltpu.roll(flat, (1 - e) % size_z, 1) if e != 1 else flat
    own = levels[1, 1, 1]
    fine = own == 1
    coarse = own != 1
    scale = jnp.where(fine, TO_COARSE, TO_FINE)
    base_time = jnp.where(fine, TAU_FINE, TAU_COARSE)
    for edge in range(3):
        for half in range(halves):
            for a, b, e in DIRECTIONS:
                over = a if a == edge and a != 1 else 1
                other = levels[over, 1, e]
                if b == 0 and half == 0:
                    other = jnp.where(sub == 0, levels[over, 0, e], other)
                if b == 2 and half == halves - 1:
                    other = jnp.where(sub == 7, levels[over, 2, e], other)
                factors[edge, half, 9 * a + 3 * b + e] = jnp.where(other != own, scale, 1.0)

    def factor_at(x, half):
        edge = (x + size_x - 1) // size_x + (x + 1) // size_x

        def factor_of(d):
            return factors[edge, half, 9 * d[0] + 3 * d[1] + d[2]]

        return factor_of

    def put(target, x, half, out):
        for d in DIRECTIONS:
            target[d[0], d[1], d[2], x + 1, pl.ds(PAD + 8 * half, 8), :] = out[d]

    def pulled(source, x, half):
        f = {}
        for a, b, e in DIRECTIONS:
            value = source[a, b, e, x + 2 - a, pl.ds(PAD + 8 * half + 1 - b, 8), :]
            f[a, b, e] = pltpu.roll(value, (e - 1) % size_z, 1) if e != 1 else value
        return f

    def held_at(x, half):
        return {
            (a, b, e): held[9 * a + 3 * b + e, x, pl.ds(8 * half, 8), :] for a, b, e in DIRECTIONS
        }

    def send(buffer, turn, side, part=0):
        a, b = side
        here_x = {0: 1, 2: size_x}
        there_x = {0: size_x + 1, 2: 0}
        here_y = {0: PAD, 2: PAD + size_y - 1}
        there_y = {0: PAD + size_y, 2: PAD - 1}
        dirs_a = pl.ds(a, 1) if a != 1 else pl.ds(0, 3)
        dirs_b = pl.ds(b, 1) if b != 1 else pl.ds(0, 3)
        along = pl.ds(1 + part * middle, middle)
        from_x = pl.ds(here_x[a], 1) if a != 1 else along
        into_x = pl.ds(there_x[a], 1) if a != 1 else along
        from_y = pl.ds(here_y[b], 1) if b != 1 else pl.ds(PAD, size_y)
        into_y = pl.ds(there_y[b], 1) if b != 1 else pl.ds(PAD, size_y)
        number = SIDES.index(side) if a != 1 else 6 + 2 * part + b // 2
        copy = pltpu.make_async_remote_copy(
            src_ref=buffer.at[dirs_a, dirs_b, :, from_x, from_y, :],
            dst_ref=buffer.at[dirs_a, dirs_b, :, into_x, into_y, :],
            send_sem=send_sem.at[turn, number],
            recv_sem=recv_sem.at[turn, number],
            device_id=(near_x[a], near_y[b]),
            device_id_type=MESH,
        )
        copy.start()
        return copy

    def send_low(buffer, turn):
        return [send(buffer, turn, (0, b)) for b in (1, 0, 2)]

    def send_high(buffer, turn):
        return [send(buffer, turn, (2, b)) for b in (1, 0, 2)]

    def send_part(buffer, turn, part):
        return [send(buffer, turn, (1, b), part) for b in (0, 2)]

    def arrived(copies):
        for copy in copies:
            copy.wait_recv()

    def first_body(x, carry):
        for half in range(halves):
            put(first, x, half, relax(held_at(x, half), base_time, coarse, factor_at(x, half)))
        return carry

    def second_body(x, carry):
        for half in range(halves):
            kept, moved = held_at(x, half), pulled(first, x, half)
            f = {d: jnp.where(fine, moved[d], kept[d]) for d in DIRECTIONS}
            put(second, x, half, relax(f, base_time, None, factor_at(x, half)))
        return carry

    loads[0].wait()
    lax.fori_loop(0, 1, first_body, 0)
    pl.semaphore_wait(barrier, len(SIDES))
    low = send_low(first, 0)
    loads[1].wait()
    lax.fori_loop(size_x - 1, size_x, first_body, 0)
    high = send_high(first, 0)
    loads[2].wait()
    lax.fori_loop(1, middle, first_body, 0)
    front = send_part(first, 0, 0)
    loads[3].wait()
    lax.fori_loop(middle, size_x - 1, first_body, 0)
    back = send_part(first, 0, 1)
    sent = low + high + front + back

    arrived(high + front)
    lax.fori_loop(0, 1, second_body, 0)
    next_low = send_low(second, 1)
    lax.fori_loop(1, middle - 1, second_body, 0)
    arrived(low + back)
    lax.fori_loop(size_x - 1, size_x, second_body, 0)
    high = send_high(second, 1)
    low = next_low
    lax.fori_loop(middle - 1, middle, second_body, 0)
    front = send_part(second, 1, 0)
    lax.fori_loop(middle, size_x - 1, second_body, 0)
    back = send_part(second, 1, 1)
    sent = sent + low + high + front + back

    curve = index_x * count_y + index_y
    home = spread([slot_ref[n] // blocks for n in range(blocks)], sub)
    to_next = home == curve + 1
    to_prev = home == curve - 1

    def last_body(x, carry):
        for half in range(halves):
            rho, momentum, _ = first_moments(pulled(second, x, half))
            inv = 1.0 / rho
            at = x * halves + half
            cells = pl.ds(pl.multiple_of(at * size_z, size_z), size_z)
            fields = [rho] + [part * inv for part in momentum]
            for n, field in enumerate(fields):
                field = swap_chunks(field, sub, chunk)
                if n == 0:
                    density_ref[:, cells] = field
                else:
                    velocity_ref[n - 1, :, cells] = field
                for mask, buffer in ((to_next, leave_next), (to_prev, leave_prev)):
                    buffer[n, pl.ds(at, 1), :] = jnp.sum(
                        jnp.where(mask, field, 0.0), axis=0, keepdims=True
                    )
        return carry

    after_x = lax.rem(index_x + (index_y + 1) // count_y, count_x)
    before_x = lax.rem(index_x + count_x - (count_y - index_y) // count_y, count_x)

    def migrate(part):
        rows = pl.ds(part * middle * halves, middle * halves)
        copies = []
        for n, (source, target, device) in enumerate(
            (
                (leave_next, come_prev, (after_x, near_y[2])),
                (leave_prev, come_next, (before_x, near_y[0])),
            )
        ):
            copy = pltpu.make_async_remote_copy(
                src_ref=source.at[:, rows],
                dst_ref=target.at[:, rows],
                send_sem=move_send.at[part, n],
                recv_sem=move_recv.at[part, n],
                device_id=device,
                device_id_type=MESH,
            )
            copy.start()
            copies.append(copy)
        return copies

    def place_body(x, carry):
        for half in range(halves):
            at = x * halves + half
            cells = pl.ds(pl.multiple_of(at * size_z, size_z), size_z)
            for n in range(4):
                old = density_ref[:, cells] if n == 0 else velocity_ref[n - 1, :, cells]
                up = jnp.broadcast_to(come_prev[n, pl.ds(at, 1), :], tile)
                down = jnp.broadcast_to(come_next[n, pl.ds(at, 1), :], tile)
                new = jnp.where(to_prev, up, jnp.where(to_next, down, old))
                if n == 0:
                    density_ref[:, cells] = new
                else:
                    velocity_ref[n - 1, :, cells] = new
        return carry

    arrived(high + front)
    lax.fori_loop(0, middle - 1, last_body, 0)
    arrived(back)
    lax.fori_loop(middle - 1, middle, last_body, 0)
    early = migrate(0)
    lax.fori_loop(middle, size_x - 1, last_body, 0)
    arrived(low)
    lax.fori_loop(size_x - 1, size_x, last_body, 0)
    late = migrate(1)
    arrived(early)
    lax.fori_loop(0, middle, place_body, 0)
    arrived(late)
    lax.fori_loop(middle, size_x, place_body, 0)
    for copy in sent + early + late:
        copy.wait_send()


def on_device(populations, block_level, new_slot):
    _, size_x, size_y, size_z = populations.shape
    blocks = new_slot.shape[0]
    sizes = (lax.axis_size("bx"), lax.axis_size("by"), size_x, size_y, size_z, blocks)
    cells = size_x * size_y * size_z // blocks
    tiles = cells // size_z
    padded = pltpu.VMEM((3, 3, 3, size_x + 2, size_y + 2 * PAD, size_z), jnp.float32)
    moving = pltpu.VMEM((4, tiles, size_z), jnp.float32)
    return pl.pallas_call(
        functools.partial(kernel, sizes),
        out_shape=(
            jax.ShapeDtypeStruct((blocks, cells), jnp.float32),
            jax.ShapeDtypeStruct((3, blocks, cells), jnp.float32),
        ),
        in_specs=[
            pl.BlockSpec(memory_space=pltpu.HBM),
            pl.BlockSpec(memory_space=pltpu.HBM),
            pl.BlockSpec(memory_space=pltpu.HBM),
        ],
        out_specs=[pl.BlockSpec(memory_space=pltpu.VMEM)] * 2,
        scratch_shapes=[
            pltpu.SMEM(block_level.shape, jnp.int32),
            pltpu.SMEM(new_slot.shape, jnp.int32),
            pltpu.VMEM(populations.shape, jnp.float32),
            padded,
            padded,
            pltpu.VMEM((3, size_y // 8, 27, 8, size_z), jnp.float32),
            moving,
            moving,
            moving,
            moving,
            pltpu.SemaphoreType.DMA((6,)),
            pltpu.SemaphoreType.DMA((2, 10)),
            pltpu.SemaphoreType.DMA((2, 10)),
            pltpu.SemaphoreType.DMA((2, 2)),
            pltpu.SemaphoreType.DMA((2, 2)),
        ],
        compiler_params=pltpu.CompilerParams(
            collective_id=0, has_side_effects=True, vmem_limit_bytes=60 * 1024 * 1024
        ),
    )(block_level, new_slot, populations)


def solution(mesh):
    in_specs = (P(None, "bx", "by", None), P(), P(("bx", "by")))
    out_specs = (P(("bx", "by"), None), P(None, ("bx", "by"), None))
    return jax.shard_map(
        on_device, mesh=mesh, in_specs=in_specs, out_specs=out_specs, check_vma=False
    )
```

```python
import functools
import math

import jax
import jax.numpy as jnp
from jax import lax
from jax.experimental import pallas as pl
from jax.experimental.pallas import tpu as pltpu
from jax.sharding import PartitionSpec as P

MESH = pl.DeviceIdType.MESH
TAU_COARSE = 0.56
TAU_FINE = 0.62
TO_FINE = TAU_FINE / (2.0 * TAU_COARSE)
TO_COARSE = 2.0 * TAU_COARSE / TAU_FINE
SMAGORINSKY = 18.0 * math.sqrt(2.0) * 0.17 * 0.17
WEIGHTS = (8.0 / 27, 2.0 / 27, 1.0 / 54, 1.0 / 216)
DIRECTIONS = [(a, b, e) for a in range(3) for b in range(3) for e in range(3)]
SIDES = [(a, b) for a in (0, 2, 1) for b in (1, 0, 2) if (a, b) != (1, 1)]
HALF = [d for d in DIRECTIONS if d > (1, 1, 1)]
PAD = 8


def opposite(direction):
    return tuple(2 - part for part in direction)


def partial_sums(f):
    ends = {(a, b): f[a, b, 0] + f[a, b, 2] for a in range(3) for b in range(3)}
    whole = {key: ends[key] + f[key + (1,)] for key in ends}
    diff = {(a, b): f[a, b, 2] - f[a, b, 0] for a in range(3) for b in range(3)}
    return ends, whole, diff


def first_moments(f):
    ends, whole, diff = partial_sums(f)
    along_x = [whole[a, 0] + whole[a, 1] + whole[a, 2] for a in range(3)]
    y_low = whole[0, 0] + whole[1, 0] + whole[2, 0]
    y_high = whole[0, 2] + whole[1, 2] + whole[2, 2]
    diff_x = [diff[a, 0] + diff[a, 1] + diff[a, 2] for a in range(3)]
    rho = along_x[0] + along_x[1] + along_x[2]
    momentum = (along_x[2] - along_x[0], y_high - y_low, diff_x[0] + diff_x[1] + diff_x[2])
    stress = (ends, whole, diff, along_x, y_low, y_high, diff_x)
    return rho, momentum, stress


def relax(f, base_time, inactive, kind_of, factor_of):
    rho, (jx, jy, jz), (ends, whole, diff, along_x, y_low, y_high, diff_x) = first_moments(f)
    pxx = along_x[0] + along_x[2]
    pyy = y_low + y_high
    pzz = ends[0, 0]
    for key in list(ends)[1:]:
        pzz = pzz + ends[key]
    pxy = (whole[2, 2] - whole[2, 0]) - (whole[0, 2] - whole[0, 0])
    pxz = diff_x[2] - diff_x[0]
    pyz = (diff[0, 2] + diff[1, 2] + diff[2, 2]) - (diff[0, 0] + diff[1, 0] + diff[2, 0])
    inv = 1.0 / rho
    ux, uy, uz = jx * inv, jy * inv, jz * inv
    third = rho * (1.0 / 3.0)
    pxx = pxx - third - jx * ux
    pyy = pyy - third - jy * uy
    pzz = pzz - third - jz * uz
    pxy = pxy - jx * uy
    pxz = pxz - jx * uz
    pyz = pyz - jy * uz
    off = pxy * pxy + pxz * pxz + pyz * pyz
    norm = jnp.sqrt(pxx * pxx + pyy * pyy + pzz * pzz + (off + off))
    tau = 0.5 * (base_time + jnp.sqrt(base_time * base_time + SMAGORINSKY * norm * inv))
    keep = 1.0 - 1.0 / tau
    if inactive is not None:
        keep = jnp.where(inactive, 1.0, keep)
    rest = 1.0 - 1.5 * (ux * ux + uy * uy + uz * uz)
    scaled = [rho * w for w in WEIGHTS]
    rests = [s * rest for s in scaled]
    squares = [s * 4.5 for s in scaled]
    linear = [s * 3.0 for s in scaled]
    out = {}
    keeps = {(1, 1, 1): keep}

    def emit(d, balance):
        kind = kind_of(d)
        if kind not in keeps:
            keeps[kind] = keep * factor_of(kind)
        out[d] = balance + (f[d] - balance) * keeps[kind]

    emit((1, 1, 1), rests[0])
    plane = {}
    for a in (1, 2):
        for b in range(3):
            if a == 1 and b == 1:
                plane[a, b] = None
            elif a == 1:
                plane[a, b] = uy if b == 2 else -uy
            else:
                plane[a, b] = ux if b == 1 else (ux + uy if b == 2 else ux - uy)
    for d in HALF:
        a, b, e = d
        level = sum(part != 1 for part in d)
        flat = plane[a, b]
        if flat is None:
            proj = uz
        elif e == 1:
            proj = flat
        else:
            proj = flat + uz if e == 2 else flat - uz
        even = rests[level] + squares[level] * (proj * proj)
        odd = linear[level] * proj
        emit(d, even + odd)
        emit(opposite(d), even - odd)
    return out


def swap_chunks(value, sub, chunk):
    lanes = value.shape[1]
    width = lanes // 8
    for k in (4, 2, 1):
        sub_bit = (sub & k) != 0
        chunk_bit = (chunk & k) != 0
        down = pltpu.roll(pltpu.roll(value, k, 0), lanes - width * k, 1)
        if k == 4:
            value = jnp.where(sub_bit != chunk_bit, down, value)
        else:
            up = pltpu.roll(pltpu.roll(value, 8 - k, 0), width * k, 1)
            value = jnp.where(
                sub_bit & ~chunk_bit, down, jnp.where(~sub_bit & chunk_bit, up, value)
            )
    return value


def kernel(
    sizes,
    level_hbm,
    slot_hbm,
    pop_ref,
    fields_ref,
    come_prev,
    come_next,
    level_ref,
    slot_ref,
    held,
    first,
    second,
    factors,
    leave_next,
    leave_prev,
    fields,
    load_sem,
    send_sem,
    recv_sem,
    move_send,
    move_recv,
    write_sem,
):
    count_x, count_y, size_x, size_y, size_z, blocks = sizes
    halves = size_y // 8
    index_x = lax.axis_index("bx")
    index_y = lax.axis_index("by")
    near_x = [lax.rem(index_x + count_x + a - 1, count_x) for a in range(3)]
    near_y = [lax.rem(index_y + count_y + b - 1, count_y) for b in range(3)]

    middle = size_x // 2
    pieces = ((0, 1), (size_x - 1, size_x), (1, middle), (middle, size_x - 1))
    loads = []
    for n, (low, high) in enumerate(pieces):
        piece = pl.ds(low, high - low)
        load = pltpu.make_async_copy(pop_ref.at[:, piece], held.at[:, piece], load_sem.at[n])
        load.start()
        loads.append(load)
    tables = [
        pltpu.make_async_copy(level_hbm, level_ref, load_sem.at[len(pieces)]),
        pltpu.make_async_copy(slot_hbm, slot_ref, load_sem.at[len(pieces) + 1]),
    ]
    for table in tables:
        table.start()

    barrier = pltpu.get_barrier_semaphore()
    for a, b in SIDES:
        pl.semaphore_signal(
            barrier, inc=1, device_id=(near_x[a], near_y[b]), device_id_type=MESH
        )

    tile = (8, size_z)
    sub = lax.broadcasted_iota(jnp.int32, tile, 0)
    lane = lax.broadcasted_iota(jnp.int32, tile, 1)
    chunk = lane // (size_z // blocks)

    def spread(values, index):
        result = jnp.full(tile, values[0], jnp.int32)
        for n in range(1, len(values)):
            result = jnp.where(index == n, values[n], result)
        return result

    for table in tables:
        table.wait()
    levels = {}
    for a in range(3):
        for b in range(3):
            begin = (near_x[a] * count_y + near_y[b]) * blocks
            flat = spread([level_ref[begin + n] for n in range(blocks)], chunk)
            for e in range(3):
                levels[a, b, e] = pltpu.roll(flat, (1 - e) % size_z, 1) if e != 1 else flat
    own = levels[1, 1, 1]
    fine = own == 1
    coarse = own != 1
    scale = jnp.where(fine, TO_COARSE, TO_FINE)
    base_time = jnp.where(fine, TAU_FINE, TAU_COARSE)
    for a, b, e in DIRECTIONS:
        other = levels[a, 1, e]
        if b == 0:
            other = jnp.where(sub == 0, levels[a, 0, e], other)
        if b == 2:
            other = jnp.where(sub == 7, levels[a, 2, e], other)
        factors[9 * a + 3 * b + e] = jnp.where(other != own, scale, 1.0)

    def kinds(edge, half):
        def kind_of(d):
            a, b, e = d
            row = b if (b == 0 and half == 0) or (b == 2 and half == halves - 1) else 1
            return (a if a == edge else 1, row, e)

        return kind_of

    def factor_of(kind):
        return factors[9 * kind[0] + 3 * kind[1] + kind[2]]

    def put(target, x, half, out):
        for d in DIRECTIONS:
            target[d[0], d[1], d[2], x + 1, pl.ds(PAD + 8 * half, 8), :] = out[d]

    def row_at(source, x, half, d):
        a, b, e = d
        return source[a, b, e, x + 2 - a, pl.ds(PAD + 8 * half + 1 - b, 8), :]

    def along_z(value, e):
        return pltpu.roll(value, (e - 1) % size_z, 1) if e != 1 else value

    def pulled(source, x, half):
        return {d: along_z(row_at(source, x, half, d), d[2]) for d in DIRECTIONS}

    def pulled_moments(source, x, half):
        parts = []
        for e in range(3):
            rows = [[row_at(source, x, half, (a, b, e)) for b in range(3)] for a in range(3)]
            xs = [rows[a][0] + rows[a][1] + rows[a][2] for a in range(3)]
            low = rows[0][0] + rows[1][0] + rows[2][0]
            high = rows[0][2] + rows[1][2] + rows[2][2]
            sums = (xs[0] + xs[1] + xs[2], xs[2] - xs[0], high - low)
            parts.append([along_z(value, e) for value in sums])
        rho, jx, jy = (parts[0][n] + parts[1][n] + parts[2][n] for n in range(3))
        return rho, (jx, jy, parts[2][0] - parts[0][0])

    def held_at(x, half):
        return {
            (a, b, e): held[9 * a + 3 * b + e, x, pl.ds(8 * half, 8), :] for a, b, e in DIRECTIONS
        }

    def send(buffer, turn, side, part=0):
        a, b = side
        here_x = {0: 1, 2: size_x}
        there_x = {0: size_x + 1, 2: 0}
        here_y = {0: PAD, 2: PAD + size_y - 1}
        there_y = {0: PAD + size_y, 2: PAD - 1}
        dirs_a = pl.ds(a, 1) if a != 1 else pl.ds(0, 3)
        dirs_b = pl.ds(b, 1) if b != 1 else pl.ds(0, 3)
        along = pl.ds(1 + part * middle, middle)
        from_x = pl.ds(here_x[a], 1) if a != 1 else along
        into_x = pl.ds(there_x[a], 1) if a != 1 else along
        from_y = pl.ds(here_y[b], 1) if b != 1 else pl.ds(PAD, size_y)
        into_y = pl.ds(there_y[b], 1) if b != 1 else pl.ds(PAD, size_y)
        number = SIDES.index(side) if a != 1 else 6 + 2 * part + b // 2
        copy = pltpu.make_async_remote_copy(
            src_ref=buffer.at[dirs_a, dirs_b, :, from_x, from_y, :],
            dst_ref=buffer.at[dirs_a, dirs_b, :, into_x, into_y, :],
            send_sem=send_sem.at[turn, number],
            recv_sem=recv_sem.at[turn, number],
            device_id=(near_x[a], near_y[b]),
            device_id_type=MESH,
        )
        copy.start()
        return copy

    def send_low(buffer, turn):
        return [send(buffer, turn, (0, b)) for b in (1, 0, 2)]

    def send_high(buffer, turn):
        return [send(buffer, turn, (2, b)) for b in (1, 0, 2)]

    def send_part(buffer, turn, part):
        return [send(buffer, turn, (1, b), part) for b in (0, 2)]

    def arrived(copies):
        for copy in copies:
            copy.wait_recv()

    def first_pass(begin, end, edge=1):
        def body(x, carry):
            for half in range(halves):
                out = relax(held_at(x, half), base_time, coarse, kinds(edge, half), factor_of)
                put(first, x, half, out)
            return carry

        lax.fori_loop(begin, end, body, 0)

    def second_pass(begin, end, edge=1):
        def body(x, carry):
            for half in range(halves):
                kept, moved = held_at(x, half), pulled(first, x, half)
                f = {d: jnp.where(fine, moved[d], kept[d]) for d in DIRECTIONS}
                put(second, x, half, relax(f, base_time, None, kinds(edge, half), factor_of))
            return carry

        lax.fori_loop(begin, end, body, 0)

    loads[0].wait()
    first_pass(0, 1, 0)
    pl.semaphore_wait(barrier, len(SIDES))
    low = send_low(first, 0)
    loads[1].wait()
    first_pass(size_x - 1, size_x, 2)
    high = send_high(first, 0)
    loads[2].wait()
    first_pass(1, middle)
    front = send_part(first, 0, 0)
    loads[3].wait()
    first_pass(middle, size_x - 1)
    back = send_part(first, 0, 1)
    sent = low + high + front + back

    arrived(high + front)
    second_pass(0, 1, 0)
    next_low = send_low(second, 1)
    second_pass(1, middle - 1)
    arrived(low + back)
    second_pass(size_x - 1, size_x, 2)
    high = send_high(second, 1)
    low = next_low
    second_pass(middle - 1, middle)
    front = send_part(second, 1, 0)
    second_pass(middle, size_x - 1)
    back = send_part(second, 1, 1)
    sent = sent + low + high + front + back

    to_next, to_prev = crossings(slot_ref, index_x * count_y + index_y, blocks, sub)

    def last_pass(begin, end):
        def body(x, carry):
            for half in range(halves):
                rho, momentum = pulled_moments(second, x, half)
                inv = 1.0 / rho
                at = x * halves + half
                cells = pl.ds(pl.multiple_of(at * size_z, size_z), size_z)
                for n, field in enumerate([rho] + [part * inv for part in momentum]):
                    field = swap_chunks(field, sub, chunk)
                    fields[n, :, cells] = field
                    for mask, buffer in ((to_next, leave_next), (to_prev, leave_prev)):
                        buffer[n, pl.ds(at, 1), :] = jnp.sum(
                            jnp.where(mask, field, 0.0), axis=0, keepdims=True
                        )
            return carry

        lax.fori_loop(begin, end, body, 0)

    after_x = lax.rem(index_x + (index_y + 1) // count_y, count_x)
    before_x = lax.rem(index_x + count_x - (count_y - index_y) // count_y, count_x)

    def migrate(part):
        rows = pl.ds(part * middle * halves, middle * halves)
        copies = []
        for n, (source, target, device) in enumerate(
            (
                (leave_next, come_prev, (after_x, near_y[2])),
                (leave_prev, come_next, (before_x, near_y[0])),
            )
        ):
            copy = pltpu.make_async_remote_copy(
                src_ref=source.at[:, rows],
                dst_ref=target.at[:, rows],
                send_sem=move_send.at[part, n],
                recv_sem=move_recv.at[part, n],
                device_id=device,
                device_id_type=MESH,
            )
            copy.start()
            copies.append(copy)
        return copies

    def write(part):
        width = middle * halves * size_z
        cells = pl.ds(part * width, width)
        copy = pltpu.make_async_copy(
            fields.at[:, :, cells], fields_ref.at[:, :, cells], write_sem.at[part]
        )
        copy.start()
        return copy

    arrived(front)
    last_pass(1, middle - 1)
    arrived(high)
    last_pass(0, 1)
    arrived(back)
    last_pass(middle - 1, middle)
    early = migrate(0)
    written = [write(0)]
    last_pass(middle, size_x - 1)
    arrived(low)
    last_pass(size_x - 1, size_x)
    late = migrate(1)
    written.append(write(1))
    for copy in sent + early + late:
        copy.wait_send()
    arrived(early + late)
    for copy in written:
        copy.wait()


def crossings(slot_ref, curve, blocks, sub):
    home = jnp.full(sub.shape, slot_ref[0] // blocks, jnp.int32)
    for n in range(1, blocks):
        home = jnp.where(sub == n, slot_ref[n] // blocks, home)
    return home == curve + 1, home == curve - 1


def place_kernel(slot_ref, fields, come_prev, come_next, density_ref, velocity_ref):
    _, tiles, width = come_prev.shape
    blocks = fields.shape[1]
    tile = (blocks, width)
    curve = lax.axis_index("bx") * lax.axis_size("by") + lax.axis_index("by")
    sub = lax.broadcasted_iota(jnp.int32, tile, 0)
    to_next, to_prev = crossings(slot_ref, curve, blocks, sub)
    for n in range(4):
        for at in range(tiles):
            cells = pl.ds(at * width, width)
            up = jnp.broadcast_to(come_prev[n, pl.ds(at, 1), :], tile)
            down = jnp.broadcast_to(come_next[n, pl.ds(at, 1), :], tile)
            new = jnp.where(to_prev, up, jnp.where(to_next, down, fields[n, :, cells]))
            if n == 0:
                density_ref[:, cells] = new
            else:
                velocity_ref[n - 1, :, cells] = new


def on_device(populations, block_level, new_slot):
    _, size_x, size_y, size_z = populations.shape
    blocks = new_slot.shape[0]
    sizes = (lax.axis_size("bx"), lax.axis_size("by"), size_x, size_y, size_z, blocks)
    cells = size_x * size_y * size_z // blocks
    tiles = cells // size_z
    padded = pltpu.VMEM((3, 3, 3, size_x + 2, size_y + 2 * PAD, size_z), jnp.float32)
    moving = (4, tiles, size_z)
    fields, come_prev, come_next = pl.pallas_call(
        functools.partial(kernel, sizes),
        out_shape=(
            jax.ShapeDtypeStruct((4, blocks, cells), jnp.float32),
            jax.ShapeDtypeStruct(moving, jnp.float32),
            jax.ShapeDtypeStruct(moving, jnp.float32),
        ),
        in_specs=[pl.BlockSpec(memory_space=pltpu.HBM)] * 3,
        out_specs=[pl.BlockSpec(memory_space=pltpu.HBM)] * 3,
        scratch_shapes=[
            pltpu.SMEM(block_level.shape, jnp.int32),
            pltpu.SMEM(new_slot.shape, jnp.int32),
            pltpu.VMEM(populations.shape, jnp.float32),
            padded,
            padded,
            pltpu.VMEM((27, 8, size_z), jnp.float32),
            pltpu.VMEM(moving, jnp.float32),
            pltpu.VMEM(moving, jnp.float32),
            pltpu.VMEM((4, blocks, cells), jnp.float32),
            pltpu.SemaphoreType.DMA((6,)),
            pltpu.SemaphoreType.DMA((2, 10)),
            pltpu.SemaphoreType.DMA((2, 10)),
            pltpu.SemaphoreType.DMA((2, 2)),
            pltpu.SemaphoreType.DMA((2, 2)),
            pltpu.SemaphoreType.DMA((2,)),
        ],
        compiler_params=pltpu.CompilerParams(
            collective_id=0, has_side_effects=True, vmem_limit_bytes=60 * 1024 * 1024
        ),
    )(block_level, new_slot, populations)
    in_vmem = pl.BlockSpec(memory_space=pltpu.VMEM)
    return pl.pallas_call(
        place_kernel,
        out_shape=(
            jax.ShapeDtypeStruct((blocks, cells), jnp.float32),
            jax.ShapeDtypeStruct((3, blocks, cells), jnp.float32),
        ),
        in_specs=[pl.BlockSpec(memory_space=pltpu.SMEM), in_vmem, in_vmem, in_vmem],
        out_specs=[in_vmem, in_vmem],
        compiler_params=pltpu.CompilerParams(vmem_limit_bytes=60 * 1024 * 1024),
    )(new_slot, fields, come_prev, come_next)


def solution(mesh):
    in_specs = (P(None, "bx", "by", None), P(), P(("bx", "by")))
    out_specs = (P(("bx", "by"), None), P(None, ("bx", "by"), None))
    return jax.shard_map(
        on_device, mesh=mesh, in_specs=in_specs, out_specs=out_specs, check_vma=False
    )
```

```python
import functools
import math

import jax
import jax.numpy as jnp
from jax import lax
from jax.experimental import pallas as pl
from jax.experimental.pallas import tpu as pltpu
from jax.sharding import PartitionSpec as P

MESH = pl.DeviceIdType.MESH
TAU_COARSE = 0.56
TAU_FINE = 0.62
TO_FINE = TAU_FINE / (2.0 * TAU_COARSE)
TO_COARSE = 2.0 * TAU_COARSE / TAU_FINE
SMAGORINSKY = 18.0 * math.sqrt(2.0) * 0.17 * 0.17
WEIGHTS = (8.0 / 27, 2.0 / 27, 1.0 / 54, 1.0 / 216)
DIRECTIONS = [(a, b, e) for a in range(3) for b in range(3) for e in range(3)]
SIDES = [(a, b) for a in (0, 2, 1) for b in (1, 0, 2) if (a, b) != (1, 1)]
HALF = [d for d in DIRECTIONS if d > (1, 1, 1)]
PAD = 8


def opposite(direction):
    return tuple(2 - part for part in direction)


def partial_sums(f):
    ends = {(a, b): f[a, b, 0] + f[a, b, 2] for a in range(3) for b in range(3)}
    whole = {key: ends[key] + f[key + (1,)] for key in ends}
    diff = {(a, b): f[a, b, 2] - f[a, b, 0] for a in range(3) for b in range(3)}
    return ends, whole, diff


def first_moments(f):
    ends, whole, diff = partial_sums(f)
    along_x = [whole[a, 0] + whole[a, 1] + whole[a, 2] for a in range(3)]
    y_low = whole[0, 0] + whole[1, 0] + whole[2, 0]
    y_high = whole[0, 2] + whole[1, 2] + whole[2, 2]
    diff_x = [diff[a, 0] + diff[a, 1] + diff[a, 2] for a in range(3)]
    rho = along_x[0] + along_x[1] + along_x[2]
    momentum = (along_x[2] - along_x[0], y_high - y_low, diff_x[0] + diff_x[1] + diff_x[2])
    stress = (ends, whole, diff, along_x, y_low, y_high, diff_x)
    return rho, momentum, stress


def settle(f, base_time, inactive):
    rho, (jx, jy, jz), (ends, whole, diff, along_x, y_low, y_high, diff_x) = first_moments(f)
    pxx = along_x[0] + along_x[2]
    pyy = y_low + y_high
    pzz = ends[0, 0]
    for key in list(ends)[1:]:
        pzz = pzz + ends[key]
    pxy = (whole[2, 2] - whole[2, 0]) - (whole[0, 2] - whole[0, 0])
    pxz = diff_x[2] - diff_x[0]
    pyz = (diff[0, 2] + diff[1, 2] + diff[2, 2]) - (diff[0, 0] + diff[1, 0] + diff[2, 0])
    inv = 1.0 / rho
    ux, uy, uz = jx * inv, jy * inv, jz * inv
    third = rho * (1.0 / 3.0)
    pxx = pxx - third - jx * ux
    pyy = pyy - third - jy * uy
    pzz = pzz - third - jz * uz
    pxy = pxy - jx * uy
    pxz = pxz - jx * uz
    pyz = pyz - jy * uz
    off = pxy * pxy + pxz * pxz + pyz * pyz
    square = pxx * pxx + pyy * pyy + pzz * pzz + (off + off)
    norm = square * lax.rsqrt(jnp.maximum(square, 1e-37))
    under = base_time * base_time + SMAGORINSKY * norm * inv
    keep = 1.0 - 2.0 / (base_time + under * lax.rsqrt(under))
    if inactive is not None:
        keep = jnp.where(inactive, 1.0, keep)
    return rho, ux, uy, uz, keep


def outgoing(settled, field_of, kind_of, factor_of, store):
    rho, ux, uy, uz, keep = settled
    rest = 1.0 - 1.5 * (ux * ux + uy * uy + uz * uz)
    scaled = [rho * w for w in WEIGHTS]
    rests = [s * rest for s in scaled]
    squares = [s * 4.5 for s in scaled]
    linear = [s * 3.0 for s in scaled]
    keeps = {(1, 1, 1): keep}

    def emit(d, balance):
        kind = kind_of(d)
        if kind not in keeps:
            keeps[kind] = keep * factor_of(kind)
        store(d, balance + (field_of(d) - balance) * keeps[kind])

    emit((1, 1, 1), rests[0])
    plane = {
        (1, 1): None,
        (1, 2): uy,
        (2, 0): ux - uy,
        (2, 1): ux,
        (2, 2): ux + uy,
    }
    for d in HALF:
        a, b, e = d
        level = sum(part != 1 for part in d)
        flat = plane[a, b]
        if flat is None:
            proj = uz
        elif e == 1:
            proj = flat
        else:
            proj = flat + uz if e == 2 else flat - uz
        even = rests[level] + squares[level] * (proj * proj)
        odd = linear[level] * proj
        emit(d, even + odd)
        emit(opposite(d), even - odd)


def swap_chunks(value, sub, chunk):
    lanes = value.shape[1]
    width = lanes // 8
    for k in (4, 2, 1):
        sub_bit = (sub & k) != 0
        chunk_bit = (chunk & k) != 0
        down = pltpu.roll(pltpu.roll(value, k, 0), lanes - width * k, 1)
        if k == 4:
            value = jnp.where(sub_bit != chunk_bit, down, value)
        else:
            up = pltpu.roll(pltpu.roll(value, 8 - k, 0), width * k, 1)
            value = jnp.where(
                sub_bit & ~chunk_bit, down, jnp.where(~sub_bit & chunk_bit, up, value)
            )
    return value


def kernel(
    sizes,
    level_hbm,
    slot_hbm,
    pop_ref,
    fields_ref,
    come_prev,
    come_next,
    level_ref,
    slot_ref,
    held,
    first,
    second,
    factors,
    leave_next,
    leave_prev,
    fields,
    load_sem,
    send_sem,
    recv_sem,
    move_send,
    move_recv,
    write_sem,
):
    count_x, count_y, size_x, size_y, size_z, blocks = sizes
    halves = size_y // 8
    index_x = lax.axis_index("bx")
    index_y = lax.axis_index("by")
    near_x = [lax.rem(index_x + count_x + a - 1, count_x) for a in range(3)]
    near_y = [lax.rem(index_y + count_y + b - 1, count_y) for b in range(3)]

    cuts = (0, size_x // 2 - 1, size_x // 2 + 3, size_x)
    pieces = ((0, 1), (size_x - 1, size_x), (1, cuts[1]), (cuts[1], cuts[2]), (cuts[2], size_x - 1))
    loads = []
    for n, (low, high) in enumerate(pieces):
        piece = pl.ds(low, high - low)
        load = pltpu.make_async_copy(pop_ref.at[:, piece], held.at[:, piece], load_sem.at[n])
        load.start()
        loads.append(load)
    tables = [
        pltpu.make_async_copy(level_hbm, level_ref, load_sem.at[len(pieces)]),
        pltpu.make_async_copy(slot_hbm, slot_ref, load_sem.at[len(pieces) + 1]),
    ]
    for table in tables:
        table.start()

    barrier = pltpu.get_barrier_semaphore()
    for a, b in SIDES:
        pl.semaphore_signal(
            barrier, inc=1, device_id=(near_x[a], near_y[b]), device_id_type=MESH
        )

    tile = (8, size_z)
    sub = lax.broadcasted_iota(jnp.int32, tile, 0)
    lane = lax.broadcasted_iota(jnp.int32, tile, 1)
    chunk = lane // (size_z // blocks)

    def spread(values, index):
        result = jnp.full(tile, values[0], jnp.int32)
        for n in range(1, len(values)):
            result = jnp.where(index == n, values[n], result)
        return result

    for table in tables:
        table.wait()
    levels = {}
    for a in range(3):
        for b in range(3):
            begin = (near_x[a] * count_y + near_y[b]) * blocks
            flat = spread([level_ref[begin + n] for n in range(blocks)], chunk)
            for e in range(3):
                levels[a, b, e] = pltpu.roll(flat, (1 - e) % size_z, 1) if e != 1 else flat
    own = levels[1, 1, 1]
    fine = own == 1
    coarse = own != 1
    scale = jnp.where(fine, TO_COARSE, TO_FINE)
    base_time = jnp.where(fine, TAU_FINE, TAU_COARSE)
    for a, b, e in DIRECTIONS:
        other = levels[a, 1, e]
        if b == 0:
            other = jnp.where(sub == 0, levels[a, 0, e], other)
        if b == 2:
            other = jnp.where(sub == 7, levels[a, 2, e], other)
        factors[9 * a + 3 * b + e] = jnp.where(other != own, scale, 1.0)

    def kinds(edge, half):
        def kind_of(d):
            a, b, e = d
            row = b if (b == 0 and half == 0) or (b == 2 and half == halves - 1) else 1
            return (a if a == edge else 1, row, e)

        return kind_of

    def factor_of(kind):
        return factors[9 * kind[0] + 3 * kind[1] + kind[2]]

    def row_at(source, x, half, d):
        a, b, e = d
        return source[a, b, e, x + 2 - a, pl.ds(PAD + 8 * half + 1 - b, 8), :]

    def along_z(value, e):
        return pltpu.roll(value, (e - 1) % size_z, 1) if e != 1 else value

    def pulled_moments(source, x, half):
        parts = []
        for e in range(3):
            rows = [[row_at(source, x, half, (a, b, e)) for b in range(3)] for a in range(3)]
            xs = [rows[a][0] + rows[a][1] + rows[a][2] for a in range(3)]
            low = rows[0][0] + rows[1][0] + rows[2][0]
            high = rows[0][2] + rows[1][2] + rows[2][2]
            sums = (xs[0] + xs[1] + xs[2], xs[2] - xs[0], high - low)
            parts.append([along_z(value, e) for value in sums])
        rho, jx, jy = (parts[0][n] + parts[1][n] + parts[2][n] for n in range(3))
        return rho, (jx, jy, parts[2][0] - parts[0][0])

    def held_row(x, half, d):
        return held[9 * d[0] + 3 * d[1] + d[2], x, pl.ds(8 * half, 8), :]

    def send(buffer, turn, side, part=0):
        a, b = side
        here_x = {0: 1, 2: size_x}
        there_x = {0: size_x + 1, 2: 0}
        here_y = {0: PAD, 2: PAD + size_y - 1}
        there_y = {0: PAD + size_y, 2: PAD - 1}
        dirs_a = pl.ds(a, 1) if a != 1 else pl.ds(0, 3)
        dirs_b = pl.ds(b, 1) if b != 1 else pl.ds(0, 3)
        along = pl.ds(1 + cuts[part], cuts[part + 1] - cuts[part])
        from_x = pl.ds(here_x[a], 1) if a != 1 else along
        into_x = pl.ds(there_x[a], 1) if a != 1 else along
        from_y = pl.ds(here_y[b], 1) if b != 1 else pl.ds(PAD, size_y)
        into_y = pl.ds(there_y[b], 1) if b != 1 else pl.ds(PAD, size_y)
        number = SIDES.index(side) if a != 1 else 6 + 2 * part + b // 2
        copy = pltpu.make_async_remote_copy(
            src_ref=buffer.at[dirs_a, dirs_b, :, from_x, from_y, :],
            dst_ref=buffer.at[dirs_a, dirs_b, :, into_x, into_y, :],
            send_sem=send_sem.at[turn, number],
            recv_sem=recv_sem.at[turn, number],
            device_id=(near_x[a], near_y[b]),
            device_id_type=MESH,
        )
        copy.start()
        return copy

    def send_low(buffer, turn):
        return [send(buffer, turn, (0, b)) for b in (1, 0, 2)]

    def send_high(buffer, turn):
        return [send(buffer, turn, (2, b)) for b in (1, 0, 2)]

    def send_part(buffer, turn, part):
        return [send(buffer, turn, (1, b), part) for b in (0, 2)]

    def arrived(copies):
        for copy in copies:
            copy.wait_recv()

    def planes(work, begin, end):
        def body(n, carry):
            x = begin + 2 * n
            work([(x, 1), (x + 1, 1)])
            return carry

        lax.fori_loop(0, (end - begin) // 2, body, 0)

    edges = [(0, 0), (size_x - 1, 2)]

    def emit_tiles(target, tiles, settled):
        for (x, half, edge), values in zip(tiles, settled):

            def field_of(d, x=x, half=half):
                return held_row(x, half, d)

            def store(d, value, x=x, half=half):
                target[d[0], d[1], d[2], x + 1, pl.ds(PAD + 8 * half, 8), :] = value

            outgoing(values, field_of, kinds(edge, half), factor_of, store)

    def first_pass(picked):
        tiles = [(x, half, edge) for x, edge in picked for half in range(halves)]
        settled = []
        for x, half, _ in tiles:
            f = {d: held_row(x, half, d) for d in DIRECTIONS}
            settled.append(settle(f, base_time, coarse))
        emit_tiles(first, tiles, settled)

    def second_pass(picked):
        tiles = [(x, half, edge) for x, edge in picked for half in range(halves)]
        settled = []
        for x, half, _ in tiles:
            f = {}
            for d in DIRECTIONS:
                moved = along_z(row_at(first, x, half, d), d[2])
                f[d] = jnp.where(fine, moved, held_row(x, half, d))
                held[9 * d[0] + 3 * d[1] + d[2], x, pl.ds(8 * half, 8), :] = f[d]
            settled.append(settle(f, base_time, None))
        emit_tiles(second, tiles, settled)

    loads[0].wait()
    loads[1].wait()
    first_pass(edges)
    pl.semaphore_wait(barrier, len(SIDES))
    low = send_low(first, 0)
    high = send_high(first, 0)
    parts = []
    begin = 1
    for part in range(3):
        end = min(cuts[part + 1], size_x - 1)
        loads[2 + part].wait()
        planes(first_pass, begin, end)
        parts.append(send_part(first, 0, part))
        begin = end
    sent = low + high + parts[0] + parts[1] + parts[2]

    arrived(parts[0])
    planes(second_pass, 1, cuts[1] - 2)
    arrived(parts[1])
    planes(second_pass, cuts[1] - 2, cuts[2] - 2)
    arrived(parts[2] + low + high)
    second_pass(edges)
    low = send_low(second, 1)
    high = send_high(second, 1)
    parts = [send_part(second, 1, 0)]
    planes(second_pass, cuts[2] - 2, cuts[2])
    parts.append(send_part(second, 1, 1))
    planes(second_pass, cuts[2], size_x - 1)
    parts.append(send_part(second, 1, 2))
    sent = sent + low + high + parts[0] + parts[1] + parts[2]

    curve = index_x * count_y + index_y
    next_row = jnp.int32(0)
    prev_row = jnp.int32(0)
    for n in range(blocks):
        next_row = jnp.where(slot_ref[n] // blocks == curve + 1, n, next_row)
        prev_row = jnp.where(slot_ref[n] // blocks == curve - 1, n, prev_row)

    def last_pass(picked):
        for x, _ in picked:
            for half in range(halves):
                rho, momentum = pulled_moments(second, x, half)
                inv = 1.0 / rho
                row = lax.rem(x + size_x - 1, size_x) * halves + half
                for n, field in enumerate([rho] + [part * inv for part in momentum]):
                    fields[n, row] = swap_chunks(field, sub, chunk)
                for n in range(4):
                    leave_next[n, pl.ds(row, 1), :] = fields[n, row, pl.ds(next_row, 1), :]
                    leave_prev[n, pl.ds(row, 1), :] = fields[n, row, pl.ds(prev_row, 1), :]

    after_x = lax.rem(index_x + (index_y + 1) // count_y, count_x)
    before_x = lax.rem(index_x + count_x - (count_y - index_y) // count_y, count_x)

    marks = (0, cuts[2] - 1, size_x)

    def migrate(part):
        rows = pl.ds(marks[part] * halves, (marks[part + 1] - marks[part]) * halves)
        copies = []
        for n, (source, target, device) in enumerate(
            (
                (leave_next, come_prev, (after_x, near_y[2])),
                (leave_prev, come_next, (before_x, near_y[0])),
            )
        ):
            copy = pltpu.make_async_remote_copy(
                src_ref=source.at[:, rows],
                dst_ref=target.at[:, rows],
                send_sem=move_send.at[part, n],
                recv_sem=move_recv.at[part, n],
                device_id=device,
                device_id_type=MESH,
            )
            copy.start()
            copies.append(copy)
        return copies

    def write(part):
        rows = pl.ds(marks[part] * halves, (marks[part + 1] - marks[part]) * halves)
        copy = pltpu.make_async_copy(
            fields.at[:, rows], fields_ref.at[:, rows], write_sem.at[part]
        )
        copy.start()
        return copy

    arrived(parts[0])
    planes(last_pass, 1, cuts[1] - 2)
    arrived(parts[1])
    planes(last_pass, cuts[1] - 2, cuts[2] - 2)
    arrived(parts[2])
    planes(last_pass, cuts[2] - 2, cuts[2])
    early = migrate(0)
    written = [write(0)]
    planes(last_pass, cuts[2], size_x - 1)
    arrived(low + high)
    last_pass(edges)
    late = migrate(1)
    written.append(write(1))
    for copy in sent + early + late:
        copy.wait_send()
    arrived(early + late)
    for copy in written:
        copy.wait()


def crossings(slot_ref, curve, blocks, sub):
    home = jnp.full(sub.shape, slot_ref[0] // blocks, jnp.int32)
    for n in range(1, blocks):
        home = jnp.where(sub == n, slot_ref[n] // blocks, home)
    return home == curve + 1, home == curve - 1


def place_kernel(first_tiles, slot_ref, fields, come_prev, come_next, density_ref, velocity_ref):
    _, tiles, width = come_prev.shape
    blocks = fields.shape[2]
    tile = (blocks, width)
    curve = lax.axis_index("bx") * lax.axis_size("by") + lax.axis_index("by")
    sub = lax.broadcasted_iota(jnp.int32, tile, 0)
    to_next, to_prev = crossings(slot_ref, curve, blocks, sub)
    for n in range(4):
        for at in range(tiles):
            cells = pl.ds(at * width, width)
            row = (at + tiles - first_tiles) % tiles
            up = jnp.broadcast_to(come_prev[n, pl.ds(row, 1), :], tile)
            down = jnp.broadcast_to(come_next[n, pl.ds(row, 1), :], tile)
            new = jnp.where(to_prev, up, jnp.where(to_next, down, fields[n, row]))
            if n == 0:
                density_ref[:, cells] = new
            else:
                velocity_ref[n - 1, :, cells] = new


def on_device(populations, block_level, new_slot):
    _, size_x, size_y, size_z = populations.shape
    blocks = new_slot.shape[0]
    sizes = (lax.axis_size("bx"), lax.axis_size("by"), size_x, size_y, size_z, blocks)
    cells = size_x * size_y * size_z // blocks
    tiles = cells // size_z
    padded = pltpu.VMEM((3, 3, 3, size_x + 2, size_y + 2 * PAD, size_z), jnp.float32)
    moving = (4, tiles, size_z)
    fields, come_prev, come_next = pl.pallas_call(
        functools.partial(kernel, sizes),
        out_shape=(
            jax.ShapeDtypeStruct((4, tiles, blocks, size_z), jnp.float32),
            jax.ShapeDtypeStruct(moving, jnp.float32),
            jax.ShapeDtypeStruct(moving, jnp.float32),
        ),
        in_specs=[pl.BlockSpec(memory_space=pltpu.HBM)] * 3,
        out_specs=[pl.BlockSpec(memory_space=pltpu.HBM)] * 3,
        scratch_shapes=[
            pltpu.SMEM(block_level.shape, jnp.int32),
            pltpu.SMEM(new_slot.shape, jnp.int32),
            pltpu.VMEM(populations.shape, jnp.float32),
            padded,
            padded,
            pltpu.VMEM((27, 8, size_z), jnp.float32),
            pltpu.VMEM(moving, jnp.float32),
            pltpu.VMEM(moving, jnp.float32),
            pltpu.VMEM((4, tiles, blocks, size_z), jnp.float32),
            pltpu.SemaphoreType.DMA((7,)),
            pltpu.SemaphoreType.DMA((2, 12)),
            pltpu.SemaphoreType.DMA((2, 12)),
            pltpu.SemaphoreType.DMA((2, 2)),
            pltpu.SemaphoreType.DMA((2, 2)),
            pltpu.SemaphoreType.DMA((2,)),
        ],
        compiler_params=pltpu.CompilerParams(
            collective_id=0, has_side_effects=True, vmem_limit_bytes=60 * 1024 * 1024
        ),
    )(block_level, new_slot, populations)
    in_vmem = pl.BlockSpec(memory_space=pltpu.VMEM)
    return pl.pallas_call(
        functools.partial(place_kernel, size_y // 8),
        out_shape=(
            jax.ShapeDtypeStruct((blocks, cells), jnp.float32),
            jax.ShapeDtypeStruct((3, blocks, cells), jnp.float32),
        ),
        in_specs=[pl.BlockSpec(memory_space=pltpu.SMEM), in_vmem, in_vmem, in_vmem],
        out_specs=[in_vmem, in_vmem],
        compiler_params=pltpu.CompilerParams(vmem_limit_bytes=60 * 1024 * 1024),
    )(new_slot, fields, come_prev, come_next)


def solution(mesh):
    in_specs = (P(None, "bx", "by", None), P(), P(("bx", "by")))
    out_specs = (P(("bx", "by"), None), P(None, ("bx", "by"), None))
    return jax.shard_map(
        on_device, mesh=mesh, in_specs=in_specs, out_specs=out_specs, check_vma=False
    )
```

```python
import functools
import math

import jax
import jax.numpy as jnp
from jax import lax
from jax.experimental import pallas as pl
from jax.experimental.pallas import tpu as pltpu
from jax.sharding import PartitionSpec as P

MESH = pl.DeviceIdType.MESH
TAU_COARSE = 0.56
TAU_FINE = 0.62
TO_FINE = TAU_FINE / (2.0 * TAU_COARSE)
TO_COARSE = 2.0 * TAU_COARSE / TAU_FINE
SMAGORINSKY = 18.0 * math.sqrt(2.0) * 0.17 * 0.17
WEIGHTS = (8.0 / 27, 2.0 / 27, 1.0 / 54, 1.0 / 216)
DIRECTIONS = [(a, b, e) for a in range(3) for b in range(3) for e in range(3)]
SIDES = [(a, b) for a in (0, 2, 1) for b in (1, 0, 2) if (a, b) != (1, 1)]
HALF = [d for d in DIRECTIONS if d > (1, 1, 1)]
PAD = 8


def opposite(direction):
    return tuple(2 - part for part in direction)


def partial_sums(f):
    ends = {(a, b): f[a, b, 0] + f[a, b, 2] for a in range(3) for b in range(3)}
    whole = {key: ends[key] + f[key + (1,)] for key in ends}
    diff = {(a, b): f[a, b, 2] - f[a, b, 0] for a in range(3) for b in range(3)}
    return ends, whole, diff


def first_moments(f):
    ends, whole, diff = partial_sums(f)
    along_x = [whole[a, 0] + whole[a, 1] + whole[a, 2] for a in range(3)]
    y_low = whole[0, 0] + whole[1, 0] + whole[2, 0]
    y_high = whole[0, 2] + whole[1, 2] + whole[2, 2]
    diff_x = [diff[a, 0] + diff[a, 1] + diff[a, 2] for a in range(3)]
    rho = along_x[0] + along_x[1] + along_x[2]
    momentum = (along_x[2] - along_x[0], y_high - y_low, diff_x[0] + diff_x[1] + diff_x[2])
    stress = (ends, whole, diff, along_x, y_low, y_high, diff_x)
    return rho, momentum, stress


def settle(f, base_time, inactive):
    rho, (jx, jy, jz), (ends, whole, diff, along_x, y_low, y_high, diff_x) = first_moments(f)
    pxx = along_x[0] + along_x[2]
    pyy = y_low + y_high
    pzz = ends[0, 0]
    for key in list(ends)[1:]:
        pzz = pzz + ends[key]
    pxy = (whole[2, 2] - whole[2, 0]) - (whole[0, 2] - whole[0, 0])
    pxz = diff_x[2] - diff_x[0]
    pyz = (diff[0, 2] + diff[1, 2] + diff[2, 2]) - (diff[0, 0] + diff[1, 0] + diff[2, 0])
    inv = 1.0 / rho
    ux, uy, uz = jx * inv, jy * inv, jz * inv
    third = rho * (1.0 / 3.0)
    pxx = pxx - third - jx * ux
    pyy = pyy - third - jy * uy
    pzz = pzz - third - jz * uz
    pxy = pxy - jx * uy
    pxz = pxz - jx * uz
    pyz = pyz - jy * uz
    off = pxy * pxy + pxz * pxz + pyz * pyz
    square = pxx * pxx + pyy * pyy + pzz * pzz + (off + off)
    norm = square * lax.rsqrt(jnp.maximum(square, 1e-37))
    under = base_time * base_time + SMAGORINSKY * norm * inv
    keep = 1.0 - 2.0 / (base_time + under * lax.rsqrt(under))
    if inactive is not None:
        keep = jnp.where(inactive, 1.0, keep)
    return rho, ux, uy, uz, keep


def outgoing(settled, field_of, kind_of, factor_of, store):
    rho, ux, uy, uz, keep = settled
    rest = 1.0 - 1.5 * (ux * ux + uy * uy + uz * uz)
    scaled = [rho * w for w in WEIGHTS]
    rests = [s * rest for s in scaled]
    squares = [s * 4.5 for s in scaled]
    linear = [s * 3.0 for s in scaled]
    keeps = {(1, 1, 1): keep}

    def emit(d, balance):
        kind = kind_of(d)
        if kind not in keeps:
            keeps[kind] = keep * factor_of(kind)
        store(d, balance + (field_of(d) - balance) * keeps[kind])

    emit((1, 1, 1), rests[0])
    plane = {
        (1, 1): None,
        (1, 2): uy,
        (2, 0): ux - uy,
        (2, 1): ux,
        (2, 2): ux + uy,
    }
    for d in HALF:
        a, b, e = d
        level = sum(part != 1 for part in d)
        flat = plane[a, b]
        if flat is None:
            proj = uz
        elif e == 1:
            proj = flat
        else:
            proj = flat + uz if e == 2 else flat - uz
        even = rests[level] + squares[level] * (proj * proj)
        odd = linear[level] * proj
        emit(d, even + odd)
        emit(opposite(d), even - odd)


def swap_chunks(value, indices):
    for axis, index in indices:
        value = jnp.take_along_axis(value, index, axis=axis, mode="promise_in_bounds")
    return value


def kernel(
    sizes,
    level_hbm,
    slot_hbm,
    pop_ref,
    fields_ref,
    come_prev,
    come_next,
    level_ref,
    slot_ref,
    held,
    first,
    second,
    factors,
    leave_next,
    leave_prev,
    fields,
    load_sem,
    send_sem,
    recv_sem,
    move_send,
    move_recv,
    write_sem,
):
    count_x, count_y, size_x, size_y, size_z, blocks = sizes
    halves = size_y // 8
    index_x = lax.axis_index("bx")
    index_y = lax.axis_index("by")
    near_x = [lax.rem(index_x + count_x + a - 1, count_x) for a in range(3)]
    near_y = [lax.rem(index_y + count_y + b - 1, count_y) for b in range(3)]

    cuts = (0, size_x // 2 - 1, size_x // 2 + 3, size_x)
    pieces = ((0, 1), (size_x - 1, size_x), (1, cuts[1]), (cuts[1], cuts[2]), (cuts[2], size_x - 1))
    loads = []
    for n, (low, high) in enumerate(pieces):
        piece = pl.ds(low, high - low)
        load = pltpu.make_async_copy(pop_ref.at[:, piece], held.at[:, piece], load_sem.at[n])
        load.start()
        loads.append(load)
    tables = [
        pltpu.make_async_copy(level_hbm, level_ref, load_sem.at[len(pieces)]),
        pltpu.make_async_copy(slot_hbm, slot_ref, load_sem.at[len(pieces) + 1]),
    ]
    for table in tables:
        table.start()

    barrier = pltpu.get_barrier_semaphore()
    for a, b in SIDES:
        pl.semaphore_signal(
            barrier, inc=1, device_id=(near_x[a], near_y[b]), device_id_type=MESH
        )

    tile = (8, size_z)
    sub = lax.broadcasted_iota(jnp.int32, tile, 0)
    lane = lax.broadcasted_iota(jnp.int32, tile, 1)
    chunk = lane // (size_z // blocks)

    def spread(values, index):
        result = jnp.full(tile, values[0], jnp.int32)
        for n in range(1, len(values)):
            result = jnp.where(index == n, values[n], result)
        return result

    for table in tables:
        table.wait()
    levels = {}
    for a in range(3):
        for b in range(3):
            begin = (near_x[a] * count_y + near_y[b]) * blocks
            flat = spread([level_ref[begin + n] for n in range(blocks)], chunk)
            for e in range(3):
                levels[a, b, e] = pltpu.roll(flat, (1 - e) % size_z, 1) if e != 1 else flat
    own = levels[1, 1, 1]
    fine = own == 1
    coarse = own != 1
    scale = jnp.where(fine, TO_COARSE, TO_FINE)
    base_time = jnp.where(fine, TAU_FINE, TAU_COARSE)
    for a, b, e in DIRECTIONS:
        other = levels[a, 1, e]
        if b == 0:
            other = jnp.where(sub == 0, levels[a, 0, e], other)
        if b == 2:
            other = jnp.where(sub == 7, levels[a, 2, e], other)
        factors[9 * a + 3 * b + e] = jnp.where(other != own, scale, 1.0)

    def kinds(edge, half):
        def kind_of(d):
            a, b, e = d
            row = b if (b == 0 and half == 0) or (b == 2 and half == halves - 1) else 1
            return (a if a == edge else 1, row, e)

        return kind_of

    def factor_of(kind):
        return factors[9 * kind[0] + 3 * kind[1] + kind[2]]

    def row_at(source, x, half, d):
        a, b, e = d
        return source[a, b, e, x + 2 - a, pl.ds(PAD + 8 * half + 1 - b, 8), :]

    def along_z(value, e):
        return pltpu.roll(value, (e - 1) % size_z, 1) if e != 1 else value

    def pulled_moments(source, x, half):
        parts = []
        for e in range(3):
            rows = [[row_at(source, x, half, (a, b, e)) for b in range(3)] for a in range(3)]
            xs = [rows[a][0] + rows[a][1] + rows[a][2] for a in range(3)]
            low = rows[0][0] + rows[1][0] + rows[2][0]
            high = rows[0][2] + rows[1][2] + rows[2][2]
            sums = (xs[0] + xs[1] + xs[2], xs[2] - xs[0], high - low)
            parts.append([along_z(value, e) for value in sums])
        rho, jx, jy = (parts[0][n] + parts[1][n] + parts[2][n] for n in range(3))
        return rho, (jx, jy, parts[2][0] - parts[0][0])

    def held_row(x, half, d):
        return held[9 * d[0] + 3 * d[1] + d[2], x, pl.ds(8 * half, 8), :]

    def send(buffer, turn, side, part=0):
        a, b = side
        here_x = {0: 1, 2: size_x}
        there_x = {0: size_x + 1, 2: 0}
        here_y = {0: PAD, 2: PAD + size_y - 1}
        there_y = {0: PAD + size_y, 2: PAD - 1}
        dirs_a = pl.ds(a, 1) if a != 1 else pl.ds(0, 3)
        dirs_b = pl.ds(b, 1) if b != 1 else pl.ds(0, 3)
        along = pl.ds(1 + cuts[part], cuts[part + 1] - cuts[part])
        from_x = pl.ds(here_x[a], 1) if a != 1 else along
        into_x = pl.ds(there_x[a], 1) if a != 1 else along
        from_y = pl.ds(here_y[b], 1) if b != 1 else pl.ds(PAD, size_y)
        into_y = pl.ds(there_y[b], 1) if b != 1 else pl.ds(PAD, size_y)
        number = SIDES.index(side) if a != 1 else 6 + 2 * part + b // 2
        copy = pltpu.make_async_remote_copy(
            src_ref=buffer.at[dirs_a, dirs_b, :, from_x, from_y, :],
            dst_ref=buffer.at[dirs_a, dirs_b, :, into_x, into_y, :],
            send_sem=send_sem.at[turn, number],
            recv_sem=recv_sem.at[turn, number],
            device_id=(near_x[a], near_y[b]),
            device_id_type=MESH,
        )
        copy.start()
        return copy

    def send_low(buffer, turn):
        return [send(buffer, turn, (0, b)) for b in (1, 0, 2)]

    def send_high(buffer, turn):
        return [send(buffer, turn, (2, b)) for b in (1, 0, 2)]

    def send_part(buffer, turn, part):
        return [send(buffer, turn, (1, b), part) for b in (0, 2)]

    def arrived(copies):
        for copy in copies:
            copy.wait_recv()

    def planes(work, begin, end):
        def body(n, carry):
            x = begin + 2 * n
            work([(x, 1), (x + 1, 1)])
            return carry

        lax.fori_loop(0, (end - begin) // 2, body, 0)

    edges = [(0, 0), (size_x - 1, 2)]

    def emit_tiles(target, tiles, settled):
        for (x, half, edge), values in zip(tiles, settled):

            def field_of(d, x=x, half=half):
                return held_row(x, half, d)

            def store(d, value, x=x, half=half):
                target[d[0], d[1], d[2], x + 1, pl.ds(PAD + 8 * half, 8), :] = value

            outgoing(values, field_of, kinds(edge, half), factor_of, store)

    def first_pass(picked):
        tiles = [(x, half, edge) for x, edge in picked for half in range(halves)]
        settled = []
        for x, half, _ in tiles:
            f = {d: held_row(x, half, d) for d in DIRECTIONS}
            settled.append(settle(f, base_time, coarse))
        emit_tiles(first, tiles, settled)

    def second_pass(picked):
        tiles = [(x, half, edge) for x, edge in picked for half in range(halves)]
        settled = []
        for x, half, _ in tiles:
            f = {}
            for d in DIRECTIONS:
                moved = along_z(row_at(first, x, half, d), d[2])
                f[d] = jnp.where(fine, moved, held_row(x, half, d))
                held[9 * d[0] + 3 * d[1] + d[2], x, pl.ds(8 * half, 8), :] = f[d]
            settled.append(settle(f, base_time, None))
        emit_tiles(second, tiles, settled)

    loads[0].wait()
    loads[1].wait()
    first_pass(edges)
    pl.semaphore_wait(barrier, len(SIDES))
    low = send_low(first, 0)
    high = send_high(first, 0)
    parts = []
    begin = 1
    for part in range(3):
        end = min(cuts[part + 1], size_x - 1)
        loads[2 + part].wait()
        planes(first_pass, begin, end)
        parts.append(send_part(first, 0, part))
        begin = end
    sent = low + high + parts[0] + parts[1] + parts[2]

    arrived(parts[0])
    planes(second_pass, 1, cuts[1] - 2)
    arrived(parts[1])
    planes(second_pass, cuts[1] - 2, cuts[2] - 2)
    arrived(parts[2] + low + high)
    second_pass(edges)
    low = send_low(second, 1)
    high = send_high(second, 1)
    parts = [send_part(second, 1, 0)]
    planes(second_pass, cuts[2] - 2, cuts[2])
    parts.append(send_part(second, 1, 1))
    planes(second_pass, cuts[2], size_x - 1)
    parts.append(send_part(second, 1, 2))
    sent = sent + low + high + parts[0] + parts[1] + parts[2]

    width = size_z // blocks
    swaps = (
        (1, (lane + sub * width) % size_z),
        (0, (sub + 8 - chunk) % 8),
        (1, ((sub + 8 - chunk) % 8) * width + lane % width),
    )
    curve = index_x * count_y + index_y
    next_row = jnp.int32(0)
    prev_row = jnp.int32(0)
    for n in range(blocks):
        next_row = jnp.where(slot_ref[n] // blocks == curve + 1, n, next_row)
        prev_row = jnp.where(slot_ref[n] // blocks == curve - 1, n, prev_row)

    def last_pass(picked):
        for x, _ in picked:
            for half in range(halves):
                rho, momentum = pulled_moments(second, x, half)
                inv = 1.0 / rho
                row = lax.rem(x + size_x - 1, size_x) * halves + half
                for n, field in enumerate([rho] + [part * inv for part in momentum]):
                    fields[n, row] = swap_chunks(field, swaps)
                for n in range(4):
                    leave_next[n, pl.ds(row, 1), :] = fields[n, row, pl.ds(next_row, 1), :]
                    leave_prev[n, pl.ds(row, 1), :] = fields[n, row, pl.ds(prev_row, 1), :]

    after_x = lax.rem(index_x + (index_y + 1) // count_y, count_x)
    before_x = lax.rem(index_x + count_x - (count_y - index_y) // count_y, count_x)

    marks = (0, cuts[2] - 1, size_x)

    def migrate(part):
        rows = pl.ds(marks[part] * halves, (marks[part + 1] - marks[part]) * halves)
        copies = []
        for n, (source, target, device) in enumerate(
            (
                (leave_next, come_prev, (after_x, near_y[2])),
                (leave_prev, come_next, (before_x, near_y[0])),
            )
        ):
            copy = pltpu.make_async_remote_copy(
                src_ref=source.at[:, rows],
                dst_ref=target.at[:, rows],
                send_sem=move_send.at[part, n],
                recv_sem=move_recv.at[part, n],
                device_id=device,
                device_id_type=MESH,
            )
            copy.start()
            copies.append(copy)
        return copies

    def write(part):
        rows = pl.ds(marks[part] * halves, (marks[part + 1] - marks[part]) * halves)
        copy = pltpu.make_async_copy(
            fields.at[:, rows], fields_ref.at[:, rows], write_sem.at[part]
        )
        copy.start()
        return copy

    arrived(parts[0])
    planes(last_pass, 1, cuts[1] - 2)
    arrived(parts[1])
    planes(last_pass, cuts[1] - 2, cuts[2] - 2)
    arrived(parts[2])
    planes(last_pass, cuts[2] - 2, cuts[2])
    early = migrate(0)
    written = [write(0)]
    planes(last_pass, cuts[2], size_x - 1)
    arrived(low + high)
    last_pass(edges)
    late = migrate(1)
    written.append(write(1))
    for copy in sent + early + late:
        copy.wait_send()
    arrived(early + late)
    for copy in written:
        copy.wait()


def crossings(slot_ref, curve, blocks, sub):
    home = jnp.full(sub.shape, slot_ref[0] // blocks, jnp.int32)
    for n in range(1, blocks):
        home = jnp.where(sub == n, slot_ref[n] // blocks, home)
    return home == curve + 1, home == curve - 1


def place_kernel(
    first_tiles,
    slot_ref,
    fields_ref,
    prev_ref,
    next_ref,
    density_ref,
    velocity_ref,
    fields,
    come_prev,
    come_next,
    placed,
    in_sem,
    out_sem,
):
    rows = [
        pltpu.make_async_copy(prev_ref, come_prev, in_sem.at[4]),
        pltpu.make_async_copy(next_ref, come_next, in_sem.at[5]),
    ]
    loads = [
        pltpu.make_async_copy(fields_ref.at[n], fields.at[n], in_sem.at[n]) for n in range(4)
    ]
    for copy in rows + loads:
        copy.start()
    _, tiles, width = come_prev.shape
    blocks = fields.shape[2]
    tile = (blocks, width)
    curve = lax.axis_index("bx") * lax.axis_size("by") + lax.axis_index("by")
    sub = lax.broadcasted_iota(jnp.int32, tile, 0)
    to_next, to_prev = crossings(slot_ref, curve, blocks, sub)
    for copy in rows:
        copy.wait()
    stores = []
    for n in range(4):
        loads[n].wait()
        for at in range(tiles):
            row = (at + tiles - first_tiles) % tiles
            up = jnp.broadcast_to(come_prev[n, pl.ds(row, 1), :], tile)
            down = jnp.broadcast_to(come_next[n, pl.ds(row, 1), :], tile)
            new = jnp.where(to_prev, up, jnp.where(to_next, down, fields[n, row]))
            placed[n, :, pl.ds(at * width, width)] = new
        target = density_ref if n == 0 else velocity_ref.at[n - 1]
        store = pltpu.make_async_copy(placed.at[n], target, out_sem.at[n])
        store.start()
        stores.append(store)
    for store in stores:
        store.wait()


def on_device(populations, block_level, new_slot):
    _, size_x, size_y, size_z = populations.shape
    blocks = new_slot.shape[0]
    sizes = (lax.axis_size("bx"), lax.axis_size("by"), size_x, size_y, size_z, blocks)
    cells = size_x * size_y * size_z // blocks
    tiles = cells // size_z
    padded = pltpu.VMEM((3, 3, 3, size_x + 2, size_y + 2 * PAD, size_z), jnp.float32)
    moving = (4, tiles, size_z)
    fields, come_prev, come_next = pl.pallas_call(
        functools.partial(kernel, sizes),
        out_shape=(
            jax.ShapeDtypeStruct((4, tiles, blocks, size_z), jnp.float32),
            jax.ShapeDtypeStruct(moving, jnp.float32),
            jax.ShapeDtypeStruct(moving, jnp.float32),
        ),
        in_specs=[pl.BlockSpec(memory_space=pltpu.HBM)] * 3,
        out_specs=[pl.BlockSpec(memory_space=pltpu.HBM)] * 3,
        scratch_shapes=[
            pltpu.SMEM(block_level.shape, jnp.int32),
            pltpu.SMEM(new_slot.shape, jnp.int32),
            pltpu.VMEM(populations.shape, jnp.float32),
            padded,
            padded,
            pltpu.VMEM((27, 8, size_z), jnp.float32),
            pltpu.VMEM(moving, jnp.float32),
            pltpu.VMEM(moving, jnp.float32),
            pltpu.VMEM((4, tiles, blocks, size_z), jnp.float32),
            pltpu.SemaphoreType.DMA((7,)),
            pltpu.SemaphoreType.DMA((2, 12)),
            pltpu.SemaphoreType.DMA((2, 12)),
            pltpu.SemaphoreType.DMA((2, 2)),
            pltpu.SemaphoreType.DMA((2, 2)),
            pltpu.SemaphoreType.DMA((2,)),
        ],
        compiler_params=pltpu.CompilerParams(
            collective_id=0, has_side_effects=True, vmem_limit_bytes=60 * 1024 * 1024
        ),
    )(block_level, new_slot, populations)
    in_hbm = pl.BlockSpec(memory_space=pltpu.HBM)
    return pl.pallas_call(
        functools.partial(place_kernel, size_y // 8),
        out_shape=(
            jax.ShapeDtypeStruct((blocks, cells), jnp.float32),
            jax.ShapeDtypeStruct((3, blocks, cells), jnp.float32),
        ),
        in_specs=[pl.BlockSpec(memory_space=pltpu.SMEM), in_hbm, in_hbm, in_hbm],
        out_specs=[in_hbm, in_hbm],
        scratch_shapes=[
            pltpu.VMEM((4, tiles, blocks, size_z), jnp.float32),
            pltpu.VMEM(moving, jnp.float32),
            pltpu.VMEM(moving, jnp.float32),
            pltpu.VMEM((4, blocks, cells), jnp.float32),
            pltpu.SemaphoreType.DMA((6,)),
            pltpu.SemaphoreType.DMA((4,)),
        ],
        compiler_params=pltpu.CompilerParams(vmem_limit_bytes=60 * 1024 * 1024),
    )(new_slot, fields, come_prev, come_next)


def solution(mesh):
    in_specs = (P(None, "bx", "by", None), P(), P(("bx", "by")))
    out_specs = (P(("bx", "by"), None), P(None, ("bx", "by"), None))
    return jax.shard_map(
        on_device, mesh=mesh, in_specs=in_specs, out_specs=out_specs, check_vma=False
    )
```

```python
import functools
import math

import jax
import jax.numpy as jnp
from jax import lax
from jax.experimental import pallas as pl
from jax.experimental.pallas import tpu as pltpu
from jax.sharding import PartitionSpec as P

MESH = pl.DeviceIdType.MESH
TAU_COARSE = 0.56
TAU_FINE = 0.62
TO_FINE = TAU_FINE / (2.0 * TAU_COARSE)
TO_COARSE = 2.0 * TAU_COARSE / TAU_FINE
SMAGORINSKY = 18.0 * math.sqrt(2.0) * 0.17 * 0.17
WEIGHTS = (8.0 / 27, 2.0 / 27, 1.0 / 54, 1.0 / 216)
DIRECTIONS = [(a, b, e) for a in range(3) for b in range(3) for e in range(3)]
SIDES = [(a, b) for a in (0, 2, 1) for b in (1, 0, 2) if (a, b) != (1, 1)]
HALF = [d for d in DIRECTIONS if d > (1, 1, 1)]
PAD = 8


def opposite(direction):
    return tuple(2 - part for part in direction)


def partial_sums(f):
    ends = {(a, b): f[a, b, 0] + f[a, b, 2] for a in range(3) for b in range(3)}
    whole = {key: ends[key] + f[key + (1,)] for key in ends}
    diff = {(a, b): f[a, b, 2] - f[a, b, 0] for a in range(3) for b in range(3)}
    return ends, whole, diff


def first_moments(f):
    ends, whole, diff = partial_sums(f)
    along_x = [whole[a, 0] + whole[a, 1] + whole[a, 2] for a in range(3)]
    y_low = whole[0, 0] + whole[1, 0] + whole[2, 0]
    y_high = whole[0, 2] + whole[1, 2] + whole[2, 2]
    diff_x = [diff[a, 0] + diff[a, 1] + diff[a, 2] for a in range(3)]
    rho = along_x[0] + along_x[1] + along_x[2]
    momentum = (along_x[2] - along_x[0], y_high - y_low, diff_x[0] + diff_x[1] + diff_x[2])
    stress = (ends, whole, diff, along_x, y_low, y_high, diff_x)
    return rho, momentum, stress


def settle(f, base_time, inactive):
    rho, (jx, jy, jz), (ends, whole, diff, along_x, y_low, y_high, diff_x) = first_moments(f)
    pxx = along_x[0] + along_x[2]
    pyy = y_low + y_high
    pzz = ends[0, 0]
    for key in list(ends)[1:]:
        pzz = pzz + ends[key]
    pxy = (whole[2, 2] - whole[2, 0]) - (whole[0, 2] - whole[0, 0])
    pxz = diff_x[2] - diff_x[0]
    pyz = (diff[0, 2] + diff[1, 2] + diff[2, 2]) - (diff[0, 0] + diff[1, 0] + diff[2, 0])
    inv = 1.0 / rho
    ux, uy, uz = jx * inv, jy * inv, jz * inv
    third = rho * (1.0 / 3.0)
    pxx = pxx - third - jx * ux
    pyy = pyy - third - jy * uy
    pzz = pzz - third - jz * uz
    pxy = pxy - jx * uy
    pxz = pxz - jx * uz
    pyz = pyz - jy * uz
    off = pxy * pxy + pxz * pxz + pyz * pyz
    square = pxx * pxx + pyy * pyy + pzz * pzz + (off + off)
    norm = square * lax.rsqrt(jnp.maximum(square, 1e-37))
    under = base_time * base_time + SMAGORINSKY * norm * inv
    keep = 1.0 - 2.0 / (base_time + under * lax.rsqrt(under))
    if inactive is not None:
        keep = jnp.where(inactive, 1.0, keep)
    return rho, ux, uy, uz, keep


def outgoing(settled, field_of, kind_of, factor_of, store):
    rho, ux, uy, uz, keep = settled
    rest = 1.0 - 1.5 * (ux * ux + uy * uy + uz * uz)
    scaled = [rho * w for w in WEIGHTS]
    rests = [s * rest for s in scaled]
    squares = [s * 4.5 for s in scaled]
    linear = [s * 3.0 for s in scaled]
    keeps = {(1, 1, 1): keep}

    def emit(d, balance):
        kind = kind_of(d)
        if kind not in keeps:
            keeps[kind] = keep * factor_of(kind)
        store(d, balance + (field_of(d) - balance) * keeps[kind])

    emit((1, 1, 1), rests[0])
    plane = {
        (1, 1): None,
        (1, 2): uy,
        (2, 0): ux - uy,
        (2, 1): ux,
        (2, 2): ux + uy,
    }
    for d in HALF:
        a, b, e = d
        level = sum(part != 1 for part in d)
        flat = plane[a, b]
        if flat is None:
            proj = uz
        elif e == 1:
            proj = flat
        else:
            proj = flat + uz if e == 2 else flat - uz
        even = rests[level] + squares[level] * (proj * proj)
        odd = linear[level] * proj
        emit(d, even + odd)
        emit(opposite(d), even - odd)


def swap_chunks(value, indices):
    for axis, index in indices:
        value = jnp.take_along_axis(value, index, axis=axis, mode="promise_in_bounds")
    return value


def kernel(
    sizes,
    level_hbm,
    slot_hbm,
    pop_ref,
    fields_ref,
    come_prev,
    come_next,
    level_ref,
    slot_ref,
    held,
    first,
    second,
    factors,
    leave_next,
    leave_prev,
    fields,
    load_sem,
    send_sem,
    recv_sem,
    move_send,
    move_recv,
    write_sem,
):
    count_x, count_y, size_x, size_y, size_z, blocks = sizes
    halves = size_y // 8
    index_x = lax.axis_index("bx")
    index_y = lax.axis_index("by")
    near_x = [lax.rem(index_x + count_x + a - 1, count_x) for a in range(3)]
    near_y = [lax.rem(index_y + count_y + b - 1, count_y) for b in range(3)]

    last = size_x - 1
    cuts = (0, 1, size_x // 2 - 1, size_x // 2 + 3, last, size_x)
    pieces = ((last, size_x), (1, cuts[2]), (cuts[2], cuts[3]), (0, 1), (cuts[3], last))
    loads = []
    for n, (low, high) in enumerate(pieces):
        piece = pl.ds(low, high - low)
        load = pltpu.make_async_copy(pop_ref.at[:, piece], held.at[:, piece], load_sem.at[n])
        load.start()
        loads.append(load)
    tables = [
        pltpu.make_async_copy(level_hbm, level_ref, load_sem.at[len(pieces)]),
        pltpu.make_async_copy(slot_hbm, slot_ref, load_sem.at[len(pieces) + 1]),
    ]
    for table in tables:
        table.start()

    barrier = pltpu.get_barrier_semaphore()
    for a, b in SIDES:
        pl.semaphore_signal(
            barrier, inc=1, device_id=(near_x[a], near_y[b]), device_id_type=MESH
        )

    tile = (8, size_z)
    sub = lax.broadcasted_iota(jnp.int32, tile, 0)
    lane = lax.broadcasted_iota(jnp.int32, tile, 1)
    chunk = lane // (size_z // blocks)

    def spread(values, index):
        result = jnp.full(tile, values[0], jnp.int32)
        for n in range(1, len(values)):
            result = jnp.where(index == n, values[n], result)
        return result

    for table in tables:
        table.wait()
    levels = {}
    for a in range(3):
        for b in range(3):
            begin = (near_x[a] * count_y + near_y[b]) * blocks
            flat = spread([level_ref[begin + n] for n in range(blocks)], chunk)
            for e in range(3):
                levels[a, b, e] = pltpu.roll(flat, (1 - e) % size_z, 1) if e != 1 else flat
    own = levels[1, 1, 1]
    fine = own == 1
    coarse = own != 1
    scale = jnp.where(fine, TO_COARSE, TO_FINE)
    base_time = jnp.where(fine, TAU_FINE, TAU_COARSE)
    for a, b, e in DIRECTIONS:
        other = levels[a, 1, e]
        if b == 0:
            other = jnp.where(sub == 0, levels[a, 0, e], other)
        if b == 2:
            other = jnp.where(sub == 7, levels[a, 2, e], other)
        factors[9 * a + 3 * b + e] = jnp.where(other != own, scale, 1.0)

    def kinds(edge, half):
        def kind_of(d):
            a, b, e = d
            row = b if (b == 0 and half == 0) or (b == 2 and half == halves - 1) else 1
            return (a if a == edge else 1, row, e)

        return kind_of

    def factor_of(kind):
        return factors[9 * kind[0] + 3 * kind[1] + kind[2]]

    def row_at(source, x, half, d):
        a, b, e = d
        return source[a, b, e, x + 2 - a, pl.ds(PAD + 8 * half + 1 - b, 8), :]

    def along_z(value, e):
        return pltpu.roll(value, (e - 1) % size_z, 1) if e != 1 else value

    def pulled_moments(source, x, half):
        parts = []
        for e in range(3):
            rows = [[row_at(source, x, half, (a, b, e)) for b in range(3)] for a in range(3)]
            xs = [rows[a][0] + rows[a][1] + rows[a][2] for a in range(3)]
            low = rows[0][0] + rows[1][0] + rows[2][0]
            high = rows[0][2] + rows[1][2] + rows[2][2]
            sums = (xs[0] + xs[1] + xs[2], xs[2] - xs[0], high - low)
            parts.append([along_z(value, e) for value in sums])
        rho, jx, jy = (parts[0][n] + parts[1][n] + parts[2][n] for n in range(3))
        return rho, (jx, jy, parts[2][0] - parts[0][0])

    def held_row(x, half, d):
        return held[9 * d[0] + 3 * d[1] + d[2], x, pl.ds(8 * half, 8), :]

    def send(buffer, turn, side, part=0):
        a, b = side
        here_x = {0: 1, 2: size_x}
        there_x = {0: size_x + 1, 2: 0}
        here_y = {0: PAD, 2: PAD + size_y - 1}
        there_y = {0: PAD + size_y, 2: PAD - 1}
        dirs_a = pl.ds(a, 1) if a != 1 else pl.ds(0, 3)
        dirs_b = pl.ds(b, 1) if b != 1 else pl.ds(0, 3)
        along = pl.ds(1 + cuts[part], cuts[part + 1] - cuts[part])
        from_x = pl.ds(here_x[a], 1) if a != 1 else along
        into_x = pl.ds(there_x[a], 1) if a != 1 else along
        from_y = pl.ds(here_y[b], 1) if b != 1 else pl.ds(PAD, size_y)
        into_y = pl.ds(there_y[b], 1) if b != 1 else pl.ds(PAD, size_y)
        number = SIDES.index(side) if a != 1 else 6 + 2 * part + b // 2
        copy = pltpu.make_async_remote_copy(
            src_ref=buffer.at[dirs_a, dirs_b, :, from_x, from_y, :],
            dst_ref=buffer.at[dirs_a, dirs_b, :, into_x, into_y, :],
            send_sem=send_sem.at[turn, number],
            recv_sem=recv_sem.at[turn, number],
            device_id=(near_x[a], near_y[b]),
            device_id_type=MESH,
        )
        copy.start()
        return copy

    def send_low(buffer, turn):
        return [send(buffer, turn, (0, b)) for b in (1, 0, 2)]

    def send_high(buffer, turn):
        return [send(buffer, turn, (2, b)) for b in (1, 0, 2)]

    def send_part(buffer, turn, part):
        return [send(buffer, turn, (1, b), part) for b in (0, 2)]

    def arrived(copies):
        for copy in copies:
            copy.wait_recv()

    def planes(work, begin, end):
        def body(n, carry):
            x = begin + 2 * n
            work([(x, 1), (x + 1, 1)])
            return carry

        lax.fori_loop(0, (end - begin) // 2, body, 0)

    low_plane = [(0, 0)]
    high_plane = [(last, 2)]

    def emit_tiles(target, tiles, settled):
        for (x, half, edge), values in zip(tiles, settled):

            def field_of(d, x=x, half=half):
                return held_row(x, half, d)

            def store(d, value, x=x, half=half):
                target[d[0], d[1], d[2], x + 1, pl.ds(PAD + 8 * half, 8), :] = value

            outgoing(values, field_of, kinds(edge, half), factor_of, store)

    def first_pass(picked):
        tiles = [(x, half, edge) for x, edge in picked for half in range(halves)]
        settled = []
        for x, half, _ in tiles:
            f = {d: held_row(x, half, d) for d in DIRECTIONS}
            settled.append(settle(f, base_time, coarse))
        emit_tiles(first, tiles, settled)

    def second_pass(picked):
        tiles = [(x, half, edge) for x, edge in picked for half in range(halves)]
        settled = []
        for x, half, _ in tiles:
            f = {}
            for d in DIRECTIONS:
                moved = along_z(row_at(first, x, half, d), d[2])
                f[d] = jnp.where(fine, moved, held_row(x, half, d))
                held[9 * d[0] + 3 * d[1] + d[2], x, pl.ds(8 * half, 8), :] = f[d]
            settled.append(settle(f, base_time, None))
        emit_tiles(second, tiles, settled)

    loads[0].wait()
    first_pass(high_plane)
    pl.semaphore_wait(barrier, len(SIDES))
    high = send_high(first, 0)
    rows = {4: send_part(first, 0, 4)}
    loads[1].wait()
    planes(first_pass, 1, cuts[2])
    rows[1] = send_part(first, 0, 1)
    loads[2].wait()
    planes(first_pass, cuts[2], cuts[3])
    rows[2] = send_part(first, 0, 2)
    loads[3].wait()
    first_pass(low_plane)
    low = send_low(first, 0)
    rows[0] = send_part(first, 0, 0)
    loads[4].wait()
    planes(first_pass, cuts[3], last)
    rows[3] = send_part(first, 0, 3)
    sent = low + high + sum(rows.values(), [])

    arrived(rows[0] + rows[1])
    planes(second_pass, 1, cuts[2] - 2)
    arrived(high)
    second_pass(low_plane)
    next_low = send_low(second, 1)
    next_rows = {0: send_part(second, 1, 0)}
    arrived(rows[2])
    planes(second_pass, cuts[2] - 2, cuts[3] - 2)
    next_rows[1] = send_part(second, 1, 1)
    arrived(rows[3] + rows[4])
    planes(second_pass, cuts[3] - 2, cuts[3])
    next_rows[2] = send_part(second, 1, 2)
    arrived(low)
    second_pass(high_plane)
    high = send_high(second, 1)
    next_rows[4] = send_part(second, 1, 4)
    planes(second_pass, cuts[3], last)
    next_rows[3] = send_part(second, 1, 3)
    low, rows = next_low, next_rows
    sent = sent + low + high + sum(rows.values(), [])

    width = size_z // blocks
    swaps = (
        (1, (lane + sub * width) % size_z),
        (0, (sub + 8 - chunk) % 8),
        (1, ((sub + 8 - chunk) % 8) * width + lane % width),
    )
    curve = index_x * count_y + index_y
    next_row = jnp.int32(0)
    prev_row = jnp.int32(0)
    for n in range(blocks):
        next_row = jnp.where(slot_ref[n] // blocks == curve + 1, n, next_row)
        prev_row = jnp.where(slot_ref[n] // blocks == curve - 1, n, prev_row)

    def last_pass(picked):
        for x, _ in picked:
            for half in range(halves):
                rho, momentum = pulled_moments(second, x, half)
                inv = 1.0 / rho
                row = lax.rem(x + size_x - 1, size_x) * halves + half
                for n, field in enumerate([rho] + [part * inv for part in momentum]):
                    fields[n, row] = swap_chunks(field, swaps)
                for n in range(4):
                    leave_next[n, pl.ds(row, 1), :] = fields[n, row, pl.ds(next_row, 1), :]
                    leave_prev[n, pl.ds(row, 1), :] = fields[n, row, pl.ds(prev_row, 1), :]

    after_x = lax.rem(index_x + (index_y + 1) // count_y, count_x)
    before_x = lax.rem(index_x + count_x - (count_y - index_y) // count_y, count_x)

    marks = (0, last, size_x)

    def migrate(part):
        rows = pl.ds(marks[part] * halves, (marks[part + 1] - marks[part]) * halves)
        copies = []
        for n, (source, target, device) in enumerate(
            (
                (leave_next, come_prev, (after_x, near_y[2])),
                (leave_prev, come_next, (before_x, near_y[0])),
            )
        ):
            copy = pltpu.make_async_remote_copy(
                src_ref=source.at[:, rows],
                dst_ref=target.at[:, rows],
                send_sem=move_send.at[part, n],
                recv_sem=move_recv.at[part, n],
                device_id=device,
                device_id_type=MESH,
            )
            copy.start()
            copies.append(copy)
        return copies

    def write(part):
        rows = pl.ds(marks[part] * halves, (marks[part + 1] - marks[part]) * halves)
        copy = pltpu.make_async_copy(
            fields.at[:, rows], fields_ref.at[:, rows], write_sem.at[part]
        )
        copy.start()
        return copy

    arrived(rows[0] + rows[1])
    planes(last_pass, 1, cuts[2] - 2)
    arrived(rows[2])
    planes(last_pass, cuts[2] - 2, cuts[3] - 2)
    arrived(rows[3] + rows[4])
    planes(last_pass, cuts[3] - 2, last)
    arrived(low)
    last_pass(high_plane)
    early = migrate(0)
    written = [write(0)]
    arrived(high)
    last_pass(low_plane)
    late = migrate(1)
    written.append(write(1))
    for copy in sent + early + late:
        copy.wait_send()
    arrived(early + late)
    for copy in written:
        copy.wait()


def crossings(slot_ref, curve, blocks, sub):
    home = jnp.full(sub.shape, slot_ref[0] // blocks, jnp.int32)
    for n in range(1, blocks):
        home = jnp.where(sub == n, slot_ref[n] // blocks, home)
    return home == curve + 1, home == curve - 1


def place_kernel(first_tiles, slot_ref, fields, come_prev, come_next, density_ref, velocity_ref):
    _, tiles, width = come_prev.shape
    blocks = fields.shape[2]
    tile = (blocks, width)
    curve = lax.axis_index("bx") * lax.axis_size("by") + lax.axis_index("by")
    sub = lax.broadcasted_iota(jnp.int32, tile, 0)
    to_next, to_prev = crossings(slot_ref, curve, blocks, sub)
    for n in range(4):
        for at in range(tiles):
            cells = pl.ds(at * width, width)
            row = (at + tiles - first_tiles) % tiles
            up = jnp.broadcast_to(come_prev[n, pl.ds(row, 1), :], tile)
            down = jnp.broadcast_to(come_next[n, pl.ds(row, 1), :], tile)
            new = jnp.where(to_prev, up, jnp.where(to_next, down, fields[n, row]))
            if n == 0:
                density_ref[:, cells] = new
            else:
                velocity_ref[n - 1, :, cells] = new


def on_device(populations, block_level, new_slot):
    _, size_x, size_y, size_z = populations.shape
    blocks = new_slot.shape[0]
    sizes = (lax.axis_size("bx"), lax.axis_size("by"), size_x, size_y, size_z, blocks)
    cells = size_x * size_y * size_z // blocks
    tiles = cells // size_z
    padded = pltpu.VMEM((3, 3, 3, size_x + 2, size_y + 2 * PAD, size_z), jnp.float32)
    moving = (4, tiles, size_z)
    fields, come_prev, come_next = pl.pallas_call(
        functools.partial(kernel, sizes),
        out_shape=(
            jax.ShapeDtypeStruct((4, tiles, blocks, size_z), jnp.float32),
            jax.ShapeDtypeStruct(moving, jnp.float32),
            jax.ShapeDtypeStruct(moving, jnp.float32),
        ),
        in_specs=[pl.BlockSpec(memory_space=pltpu.HBM)] * 3,
        out_specs=[pl.BlockSpec(memory_space=pltpu.HBM)] * 3,
        scratch_shapes=[
            pltpu.SMEM(block_level.shape, jnp.int32),
            pltpu.SMEM(new_slot.shape, jnp.int32),
            pltpu.VMEM(populations.shape, jnp.float32),
            padded,
            padded,
            pltpu.VMEM((27, 8, size_z), jnp.float32),
            pltpu.VMEM(moving, jnp.float32),
            pltpu.VMEM(moving, jnp.float32),
            pltpu.VMEM((4, tiles, blocks, size_z), jnp.float32),
            pltpu.SemaphoreType.DMA((7,)),
            pltpu.SemaphoreType.DMA((2, 16)),
            pltpu.SemaphoreType.DMA((2, 16)),
            pltpu.SemaphoreType.DMA((2, 2)),
            pltpu.SemaphoreType.DMA((2, 2)),
            pltpu.SemaphoreType.DMA((2,)),
        ],
        compiler_params=pltpu.CompilerParams(
            collective_id=0, has_side_effects=True, vmem_limit_bytes=60 * 1024 * 1024
        ),
    )(block_level, new_slot, populations)
    in_vmem = pl.BlockSpec(memory_space=pltpu.VMEM)
    return pl.pallas_call(
        functools.partial(place_kernel, size_y // 8),
        out_shape=(
            jax.ShapeDtypeStruct((blocks, cells), jnp.float32),
            jax.ShapeDtypeStruct((3, blocks, cells), jnp.float32),
        ),
        in_specs=[pl.BlockSpec(memory_space=pltpu.SMEM), in_vmem, in_vmem, in_vmem],
        out_specs=[in_vmem, in_vmem],
        compiler_params=pltpu.CompilerParams(vmem_limit_bytes=60 * 1024 * 1024),
    )(new_slot, fields, come_prev, come_next)


def solution(mesh):
    in_specs = (P(None, "bx", "by", None), P(), P(("bx", "by")))
    out_specs = (P(("bx", "by"), None), P(None, ("bx", "by"), None))
    return jax.shard_map(
        on_device, mesh=mesh, in_specs=in_specs, out_specs=out_specs, check_vma=False
    )
```

```python
import functools
import math

import jax
import jax.numpy as jnp
from jax import lax
from jax.experimental import pallas as pl
from jax.experimental.pallas import tpu as pltpu
from jax.sharding import PartitionSpec as P

MESH = pl.DeviceIdType.MESH
TAU_COARSE = 0.56
TAU_FINE = 0.62
TO_FINE = TAU_FINE / (2.0 * TAU_COARSE)
TO_COARSE = 2.0 * TAU_COARSE / TAU_FINE
SMAGORINSKY = 18.0 * math.sqrt(2.0) * 0.17 * 0.17
WEIGHTS = (8.0 / 27, 2.0 / 27, 1.0 / 54, 1.0 / 216)
DIRECTIONS = [(a, b, e) for a in range(3) for b in range(3) for e in range(3)]
SIDES = [(a, b) for a in (0, 2, 1) for b in (1, 0, 2) if (a, b) != (1, 1)]
HALF = [d for d in DIRECTIONS if d > (1, 1, 1)]
PAD = 8


def opposite(direction):
    return tuple(2 - part for part in direction)


def partial_sums(f):
    ends = {(a, b): f[a, b, 0] + f[a, b, 2] for a in range(3) for b in range(3)}
    whole = {key: ends[key] + f[key + (1,)] for key in ends}
    diff = {(a, b): f[a, b, 2] - f[a, b, 0] for a in range(3) for b in range(3)}
    return ends, whole, diff


def first_moments(f):
    ends, whole, diff = partial_sums(f)
    along_x = [whole[a, 0] + whole[a, 1] + whole[a, 2] for a in range(3)]
    y_low = whole[0, 0] + whole[1, 0] + whole[2, 0]
    y_high = whole[0, 2] + whole[1, 2] + whole[2, 2]
    diff_x = [diff[a, 0] + diff[a, 1] + diff[a, 2] for a in range(3)]
    rho = along_x[0] + along_x[1] + along_x[2]
    momentum = (along_x[2] - along_x[0], y_high - y_low, diff_x[0] + diff_x[1] + diff_x[2])
    stress = (ends, whole, diff, along_x, y_low, y_high, diff_x)
    return rho, momentum, stress


def settle(f, base_time, inactive):
    rho, (jx, jy, jz), (ends, whole, diff, along_x, y_low, y_high, diff_x) = first_moments(f)
    pxx = along_x[0] + along_x[2]
    pyy = y_low + y_high
    pzz = ends[0, 0]
    for key in list(ends)[1:]:
        pzz = pzz + ends[key]
    pxy = (whole[2, 2] - whole[2, 0]) - (whole[0, 2] - whole[0, 0])
    pxz = diff_x[2] - diff_x[0]
    pyz = (diff[0, 2] + diff[1, 2] + diff[2, 2]) - (diff[0, 0] + diff[1, 0] + diff[2, 0])
    inv = 1.0 / rho
    ux, uy, uz = jx * inv, jy * inv, jz * inv
    third = rho * (1.0 / 3.0)
    pxx = pxx - third - jx * ux
    pyy = pyy - third - jy * uy
    pzz = pzz - third - jz * uz
    pxy = pxy - jx * uy
    pxz = pxz - jx * uz
    pyz = pyz - jy * uz
    off = pxy * pxy + pxz * pxz + pyz * pyz
    square = pxx * pxx + pyy * pyy + pzz * pzz + (off + off)
    norm = square * lax.rsqrt(jnp.maximum(square, 1e-37))
    under = base_time * base_time + SMAGORINSKY * norm * inv
    keep = 1.0 - 2.0 / (base_time + under * lax.rsqrt(under))
    if inactive is not None:
        keep = jnp.where(inactive, 1.0, keep)
    return rho, ux, uy, uz, keep


def outgoing(settled, field_of, kind_of, factor_of, store):
    rho, ux, uy, uz, keep = settled
    rest = 1.0 - 1.5 * (ux * ux + uy * uy + uz * uz)
    scaled = [rho * w for w in WEIGHTS]
    rests = [s * rest for s in scaled]
    squares = [s * 4.5 for s in scaled]
    linear = [s * 3.0 for s in scaled]
    keeps = {(1, 1, 1): keep}

    def emit(d, balance):
        kind = kind_of(d)
        if kind not in keeps:
            keeps[kind] = keep * factor_of(kind)
        store(d, balance + (field_of(d) - balance) * keeps[kind])

    emit((1, 1, 1), rests[0])
    plane = {
        (1, 1): None,
        (1, 2): uy,
        (2, 0): ux - uy,
        (2, 1): ux,
        (2, 2): ux + uy,
    }
    for d in HALF:
        a, b, e = d
        level = sum(part != 1 for part in d)
        flat = plane[a, b]
        if flat is None:
            proj = uz
        elif e == 1:
            proj = flat
        else:
            proj = flat + uz if e == 2 else flat - uz
        even = rests[level] + squares[level] * (proj * proj)
        odd = linear[level] * proj
        emit(d, even + odd)
        emit(opposite(d), even - odd)


def swap_chunks(value, indices):
    for axis, index in indices:
        value = jnp.take_along_axis(value, index, axis=axis, mode="promise_in_bounds")
    return value


def kernel(
    sizes,
    level_hbm,
    slot_hbm,
    pop_ref,
    fields_ref,
    come_prev,
    come_next,
    level_ref,
    slot_ref,
    held,
    first,
    second,
    factors,
    leave_next,
    leave_prev,
    fields,
    load_sem,
    send_sem,
    recv_sem,
    move_send,
    move_recv,
    write_sem,
):
    count_x, count_y, size_x, size_y, size_z, blocks = sizes
    halves = size_y // 8
    index_x = lax.axis_index("bx")
    index_y = lax.axis_index("by")
    near_x = [lax.rem(index_x + count_x + a - 1, count_x) for a in range(3)]
    near_y = [lax.rem(index_y + count_y + b - 1, count_y) for b in range(3)]

    last = size_x - 1
    cuts = (0, 1, size_x // 2 - 1, size_x // 2 + 3, size_x // 2 + 5, last, size_x)
    pieces = ((last, size_x), (1, cuts[2]), (cuts[2], cuts[3]), (0, 1), (cuts[3], last))
    loads = []
    for n, (low, high) in enumerate(pieces):
        piece = pl.ds(low, high - low)
        load = pltpu.make_async_copy(pop_ref.at[:, piece], held.at[:, piece], load_sem.at[n])
        load.start()
        loads.append(load)
    tables = [
        pltpu.make_async_copy(level_hbm, level_ref, load_sem.at[len(pieces)]),
        pltpu.make_async_copy(slot_hbm, slot_ref, load_sem.at[len(pieces) + 1]),
    ]
    for table in tables:
        table.start()

    barrier = pltpu.get_barrier_semaphore()
    for a, b in SIDES:
        pl.semaphore_signal(
            barrier, inc=1, device_id=(near_x[a], near_y[b]), device_id_type=MESH
        )

    tile = (8, size_z)
    sub = lax.broadcasted_iota(jnp.int32, tile, 0)
    lane = lax.broadcasted_iota(jnp.int32, tile, 1)
    chunk = lane // (size_z // blocks)

    def spread(values, index):
        result = jnp.full(tile, values[0], jnp.int32)
        for n in range(1, len(values)):
            result = jnp.where(index == n, values[n], result)
        return result

    for table in tables:
        table.wait()
    levels = {}
    for a in range(3):
        for b in range(3):
            begin = (near_x[a] * count_y + near_y[b]) * blocks
            flat = spread([level_ref[begin + n] for n in range(blocks)], chunk)
            for e in range(3):
                levels[a, b, e] = pltpu.roll(flat, (1 - e) % size_z, 1) if e != 1 else flat
    own = levels[1, 1, 1]
    fine = own == 1
    coarse = own != 1
    scale = jnp.where(fine, TO_COARSE, TO_FINE)
    base_time = jnp.where(fine, TAU_FINE, TAU_COARSE)
    for a, b, e in DIRECTIONS:
        other = levels[a, 1, e]
        if b == 0:
            other = jnp.where(sub == 0, levels[a, 0, e], other)
        if b == 2:
            other = jnp.where(sub == 7, levels[a, 2, e], other)
        factors[9 * a + 3 * b + e] = jnp.where(other != own, scale, 1.0)

    def kinds(edge, half):
        def kind_of(d):
            a, b, e = d
            row = b if (b == 0 and half == 0) or (b == 2 and half == halves - 1) else 1
            return (a if a == edge else 1, row, e)

        return kind_of

    def factor_of(kind):
        return factors[9 * kind[0] + 3 * kind[1] + kind[2]]

    def row_at(source, x, half, d):
        a, b, e = d
        return source[a, b, e, x + 2 - a, pl.ds(PAD + 8 * half + 1 - b, 8), :]

    def along_z(value, e):
        return pltpu.roll(value, (e - 1) % size_z, 1) if e != 1 else value

    def pulled_moments(source, x, half):
        parts = []
        for e in range(3):
            rows = [[row_at(source, x, half, (a, b, e)) for b in range(3)] for a in range(3)]
            xs = [rows[a][0] + rows[a][1] + rows[a][2] for a in range(3)]
            low = rows[0][0] + rows[1][0] + rows[2][0]
            high = rows[0][2] + rows[1][2] + rows[2][2]
            sums = (xs[0] + xs[1] + xs[2], xs[2] - xs[0], high - low)
            parts.append([along_z(value, e) for value in sums])
        rho, jx, jy = (parts[0][n] + parts[1][n] + parts[2][n] for n in range(3))
        return rho, (jx, jy, parts[2][0] - parts[0][0])

    def held_row(x, half, d):
        return held[9 * d[0] + 3 * d[1] + d[2], x, pl.ds(8 * half, 8), :]

    def send(buffer, turn, side, part=0):
        a, b = side
        here_x = {0: 1, 2: size_x}
        there_x = {0: size_x + 1, 2: 0}
        here_y = {0: PAD, 2: PAD + size_y - 1}
        there_y = {0: PAD + size_y, 2: PAD - 1}
        dirs_a = pl.ds(a, 1) if a != 1 else pl.ds(0, 3)
        dirs_b = pl.ds(b, 1) if b != 1 else pl.ds(0, 3)
        along = pl.ds(1 + cuts[part], cuts[part + 1] - cuts[part])
        from_x = pl.ds(here_x[a], 1) if a != 1 else along
        into_x = pl.ds(there_x[a], 1) if a != 1 else along
        from_y = pl.ds(here_y[b], 1) if b != 1 else pl.ds(PAD, size_y)
        into_y = pl.ds(there_y[b], 1) if b != 1 else pl.ds(PAD, size_y)
        number = SIDES.index(side) if a != 1 else 6 + 2 * part + b // 2
        copy = pltpu.make_async_remote_copy(
            src_ref=buffer.at[dirs_a, dirs_b, :, from_x, from_y, :],
            dst_ref=buffer.at[dirs_a, dirs_b, :, into_x, into_y, :],
            send_sem=send_sem.at[turn, number],
            recv_sem=recv_sem.at[turn, number],
            device_id=(near_x[a], near_y[b]),
            device_id_type=MESH,
        )
        copy.start()
        return copy

    def send_low(buffer, turn):
        return [send(buffer, turn, (0, b)) for b in (1, 0, 2)]

    def send_high(buffer, turn):
        return [send(buffer, turn, (2, b)) for b in (1, 0, 2)]

    def send_part(buffer, turn, part):
        return [send(buffer, turn, (1, b), part) for b in (0, 2)]

    def arrived(copies):
        for copy in copies:
            copy.wait_recv()

    def planes(work, begin, end):
        def body(n, carry):
            x = begin + 2 * n
            work([(x, 1), (x + 1, 1)])
            return carry

        lax.fori_loop(0, (end - begin) // 2, body, 0)

    low_plane = [(0, 0)]
    high_plane = [(last, 2)]

    def emit_tiles(target, tiles, settled):
        for (x, half, edge), values in zip(tiles, settled):

            def field_of(d, x=x, half=half):
                return held_row(x, half, d)

            def store(d, value, x=x, half=half):
                target[d[0], d[1], d[2], x + 1, pl.ds(PAD + 8 * half, 8), :] = value

            outgoing(values, field_of, kinds(edge, half), factor_of, store)

    def first_pass(picked):
        tiles = [(x, half, edge) for x, edge in picked for half in range(halves)]
        settled = []
        for x, half, _ in tiles:
            f = {d: held_row(x, half, d) for d in DIRECTIONS}
            settled.append(settle(f, base_time, coarse))
        emit_tiles(first, tiles, settled)

    def second_pass(picked):
        tiles = [(x, half, edge) for x, edge in picked for half in range(halves)]
        settled = []
        for x, half, _ in tiles:
            f = {}
            for d in DIRECTIONS:
                moved = along_z(row_at(first, x, half, d), d[2])
                f[d] = jnp.where(fine, moved, held_row(x, half, d))
                held[9 * d[0] + 3 * d[1] + d[2], x, pl.ds(8 * half, 8), :] = f[d]
            settled.append(settle(f, base_time, None))
        emit_tiles(second, tiles, settled)

    loads[0].wait()
    first_pass(high_plane)
    pl.semaphore_wait(barrier, len(SIDES))
    high = send_high(first, 0)
    rows = {5: send_part(first, 0, 5)}
    loads[1].wait()
    planes(first_pass, 1, cuts[2])
    rows[1] = send_part(first, 0, 1)
    loads[2].wait()
    planes(first_pass, cuts[2], cuts[3])
    rows[2] = send_part(first, 0, 2)
    loads[3].wait()
    first_pass(low_plane)
    low = send_low(first, 0)
    rows[0] = send_part(first, 0, 0)
    loads[4].wait()
    planes(first_pass, cuts[3], cuts[4])
    rows[3] = send_part(first, 0, 3)
    planes(first_pass, cuts[4], last)
    rows[4] = send_part(first, 0, 4)
    sent = low + high + sum(rows.values(), [])

    arrived(rows[0] + rows[1])
    planes(second_pass, 1, cuts[2] - 2)
    arrived(high)
    second_pass(low_plane)
    next_low = send_low(second, 1)
    next_rows = {0: send_part(second, 1, 0)}
    arrived(rows[2])
    planes(second_pass, cuts[2] - 2, cuts[3] - 2)
    next_rows[1] = send_part(second, 1, 1)
    arrived(rows[3])
    planes(second_pass, cuts[3] - 2, cuts[3])
    next_rows[2] = send_part(second, 1, 2)
    arrived(rows[4] + rows[5] + low)
    second_pass(high_plane)
    high = send_high(second, 1)
    next_rows[5] = send_part(second, 1, 5)
    planes(second_pass, cuts[3], cuts[4])
    next_rows[3] = send_part(second, 1, 3)
    planes(second_pass, cuts[4], last)
    next_rows[4] = send_part(second, 1, 4)
    low, rows = next_low, next_rows
    sent = sent + low + high + sum(rows.values(), [])

    width = size_z // blocks
    swaps = (
        (1, (lane + sub * width) % size_z),
        (0, (sub + 8 - chunk) % 8),
        (1, ((sub + 8 - chunk) % 8) * width + lane % width),
    )
    curve = index_x * count_y + index_y
    next_row = jnp.int32(0)
    prev_row = jnp.int32(0)
    for n in range(blocks):
        next_row = jnp.where(slot_ref[n] // blocks == curve + 1, n, next_row)
        prev_row = jnp.where(slot_ref[n] // blocks == curve - 1, n, prev_row)

    def last_pass(picked):
        for x, _ in picked:
            for half in range(halves):
                rho, momentum = pulled_moments(second, x, half)
                inv = 1.0 / rho
                row = lax.rem(x + size_x - 1, size_x) * halves + half
                for n, field in enumerate([rho] + [part * inv for part in momentum]):
                    fields[n, row] = swap_chunks(field, swaps)
                for n in range(4):
                    leave_next[n, pl.ds(row, 1), :] = fields[n, row, pl.ds(next_row, 1), :]
                    leave_prev[n, pl.ds(row, 1), :] = fields[n, row, pl.ds(prev_row, 1), :]

    after_x = lax.rem(index_x + (index_y + 1) // count_y, count_x)
    before_x = lax.rem(index_x + count_x - (count_y - index_y) // count_y, count_x)

    marks = (0, cuts[3] - 1, size_x)

    def migrate(part):
        rows = pl.ds(marks[part] * halves, (marks[part + 1] - marks[part]) * halves)
        copies = []
        for n, (source, target, device) in enumerate(
            (
                (leave_next, come_prev, (after_x, near_y[2])),
                (leave_prev, come_next, (before_x, near_y[0])),
            )
        ):
            copy = pltpu.make_async_remote_copy(
                src_ref=source.at[:, rows],
                dst_ref=target.at[:, rows],
                send_sem=move_send.at[part, n],
                recv_sem=move_recv.at[part, n],
                device_id=device,
                device_id_type=MESH,
            )
            copy.start()
            copies.append(copy)
        return copies

    def write(part):
        rows = pl.ds(marks[part] * halves, (marks[part + 1] - marks[part]) * halves)
        copy = pltpu.make_async_copy(
            fields.at[:, rows], fields_ref.at[:, rows], write_sem.at[part]
        )
        copy.start()
        return copy

    arrived(rows[0] + rows[1])
    planes(last_pass, 1, cuts[2] - 2)
    arrived(rows[2])
    planes(last_pass, cuts[2] - 2, cuts[3] - 2)
    arrived(rows[3])
    planes(last_pass, cuts[3] - 2, cuts[3])
    early = migrate(0)
    written = [write(0)]
    arrived(rows[4] + rows[5])
    planes(last_pass, cuts[3], last)
    arrived(low)
    last_pass(high_plane)
    arrived(high)
    last_pass(low_plane)
    late = migrate(1)
    written.append(write(1))
    for copy in sent + early + late:
        copy.wait_send()
    arrived(early + late)
    for copy in written:
        copy.wait()


def crossings(slot_ref, curve, blocks, sub):
    home = jnp.full(sub.shape, slot_ref[0] // blocks, jnp.int32)
    for n in range(1, blocks):
        home = jnp.where(sub == n, slot_ref[n] // blocks, home)
    return home == curve + 1, home == curve - 1


def place_kernel(first_tiles, slot_ref, fields, come_prev, come_next, density_ref, velocity_ref):
    _, tiles, width = come_prev.shape
    blocks = fields.shape[2]
    tile = (blocks, width)
    curve = lax.axis_index("bx") * lax.axis_size("by") + lax.axis_index("by")
    sub = lax.broadcasted_iota(jnp.int32, tile, 0)
    to_next, to_prev = crossings(slot_ref, curve, blocks, sub)
    for n in range(4):
        for at in range(tiles):
            cells = pl.ds(at * width, width)
            row = (at + tiles - first_tiles) % tiles
            up = jnp.broadcast_to(come_prev[n, pl.ds(row, 1), :], tile)
            down = jnp.broadcast_to(come_next[n, pl.ds(row, 1), :], tile)
            new = jnp.where(to_prev, up, jnp.where(to_next, down, fields[n, row]))
            if n == 0:
                density_ref[:, cells] = new
            else:
                velocity_ref[n - 1, :, cells] = new


def on_device(populations, block_level, new_slot):
    _, size_x, size_y, size_z = populations.shape
    blocks = new_slot.shape[0]
    sizes = (lax.axis_size("bx"), lax.axis_size("by"), size_x, size_y, size_z, blocks)
    cells = size_x * size_y * size_z // blocks
    tiles = cells // size_z
    padded = pltpu.VMEM((3, 3, 3, size_x + 2, size_y + 2 * PAD, size_z), jnp.float32)
    moving = (4, tiles, size_z)
    fields, come_prev, come_next = pl.pallas_call(
        functools.partial(kernel, sizes),
        out_shape=(
            jax.ShapeDtypeStruct((4, tiles, blocks, size_z), jnp.float32),
            jax.ShapeDtypeStruct(moving, jnp.float32),
            jax.ShapeDtypeStruct(moving, jnp.float32),
        ),
        in_specs=[pl.BlockSpec(memory_space=pltpu.HBM)] * 3,
        out_specs=[pl.BlockSpec(memory_space=pltpu.HBM)] * 3,
        scratch_shapes=[
            pltpu.SMEM(block_level.shape, jnp.int32),
            pltpu.SMEM(new_slot.shape, jnp.int32),
            pltpu.VMEM(populations.shape, jnp.float32),
            padded,
            padded,
            pltpu.VMEM((27, 8, size_z), jnp.float32),
            pltpu.VMEM(moving, jnp.float32),
            pltpu.VMEM(moving, jnp.float32),
            pltpu.VMEM((4, tiles, blocks, size_z), jnp.float32),
            pltpu.SemaphoreType.DMA((7,)),
            pltpu.SemaphoreType.DMA((2, 18)),
            pltpu.SemaphoreType.DMA((2, 18)),
            pltpu.SemaphoreType.DMA((2, 2)),
            pltpu.SemaphoreType.DMA((2, 2)),
            pltpu.SemaphoreType.DMA((2,)),
        ],
        compiler_params=pltpu.CompilerParams(
            collective_id=0, has_side_effects=True, vmem_limit_bytes=60 * 1024 * 1024
        ),
    )(block_level, new_slot, populations)
    in_vmem = pl.BlockSpec(memory_space=pltpu.VMEM)
    return pl.pallas_call(
        functools.partial(place_kernel, size_y // 8),
        out_shape=(
            jax.ShapeDtypeStruct((blocks, cells), jnp.float32),
            jax.ShapeDtypeStruct((3, blocks, cells), jnp.float32),
        ),
        in_specs=[pl.BlockSpec(memory_space=pltpu.SMEM), in_vmem, in_vmem, in_vmem],
        out_specs=[in_vmem, in_vmem],
        compiler_params=pltpu.CompilerParams(vmem_limit_bytes=60 * 1024 * 1024),
    )(new_slot, fields, come_prev, come_next)


def solution(mesh):
    in_specs = (P(None, "bx", "by", None), P(), P(("bx", "by")))
    out_specs = (P(("bx", "by"), None), P(None, ("bx", "by"), None))
    return jax.shard_map(
        on_device, mesh=mesh, in_specs=in_specs, out_specs=out_specs, check_vma=False
    )
```
